512 devices in a mesh: rows: 128 (over z, y, core), panel: 4 (over x).
Axes of the slice: x: 4, y: 8, z: 8, core: 2. Of those that a mesh axis runs over, the one named last changes fastest.
Arguments:
- columns: float32 [256, 524288], P('panel', 'rows'), as said below
- pivots: int32 [256], replicated, may hold values from 0 to 524287, as said below
- start: float32 [256, 32], replicated, may hold values from -6 to 6
Outputs:
- volumes: float32 [32, 524288], P(None, ('rows', 'panel'))
The draws below stay inside these ranges and needn't reach their ends.
Inputs may be any that keep to these rules, and one draw needn't show every extreme that they name: `pivots`: distinct voxel indices; index 0 and 524287 are always among them; the voxel shards hold very unequal numbers of them. `columns`: real-valued entries.
All inputs are finite; a program needn't handle non-finite values.
Results may differ from the reference program's by a relative error of at most 0.003.
Values sent between devices are 32-bit elements; how exact they have to be, the bound alone decides.
No kernel may reach another device: no remote copies, remote signals or barrier semaphores. Data moves between devices by JAX's collectives and lax.ppermute only.
A program may use at most 64 MiB of HBM per device.

```python
import math
import jax
import jax.numpy as jnp
from jax import lax

K = 256
R = 32
VDEV = 4096
ITERS = 3
VOX = 524288
N_ROWS = 128


def draw_columns(key, part):
    key = jax.random.fold_in(key, 11)
    key_mix, key_lat, key_noise, key_cols = jax.random.split(key, 4)
    mixing = jax.random.normal(key_mix, (K, R), jnp.float32) / math.sqrt(R)
    column_scale = jnp.exp(jax.random.uniform(key_cols, (K, 1), jnp.float32, 0.0, math.log(2.0)))
    latent = jax.random.normal(key_lat, (R, VOX), jnp.float32)
    noise_part = jax.random.normal(key_noise, (K, VOX), jnp.float32)
    summed = noise_part
    for member in range(R):
        summed = summed + 2.0 * mixing[:, member:member + 1] * latent[member:member + 1, :]
    return (summed * column_scale).astype(jnp.float32)


def draw_pivots(key, part):
    key = jax.random.fold_in(key, 23)
    key_a, key_b, key_c = jax.random.split(key, 3)
    stride = VDEV // K
    first = jax.random.randint(key_a, (K,), 0, N_ROWS)
    second = jax.random.randint(key_b, (K,), 0, N_ROWS)
    owner = jnp.minimum(jnp.minimum(first, second), jax.random.randint(key_c, (K,), 0, N_ROWS))
    spot = jax.random.randint(jax.random.fold_in(key_c, 5), (K,), 0, stride)
    place = jnp.arange(K, dtype=jnp.int32)
    owner = jnp.where(place == 0, 0, jnp.where(place == K - 1, N_ROWS - 1, owner))
    spot = jnp.where(place == 0, 0, jnp.where(place == K - 1, stride - 1, spot))
    return (owner * VDEV + place * stride + spot).astype(jnp.int32)


def scatter_about(own_key, shape, deviation, bound, kind=jnp.bfloat16):
    result = deviation * jax.random.normal(own_key, shape, jnp.float32)
    return jnp.clip(result, min=-bound, max=bound).astype(kind)


def setup_inputs(seed: int = 0) -> dict:
    key_of = jax.random.split(jax.random.key(seed), 4)
    return {
        "columns": draw_columns(jax.random.fold_in(key_of[3], 71), 0),
        "pivots": draw_pivots(jax.random.fold_in(key_of[3], 71), 0),
        "start": scatter_about(key_of[2], (K, R), 1.0, 6.0, jnp.float32),
    }


core_shift = 0.1

def lower_solve(factor, rhs):
    return lax.linalg.triangular_solve(factor, rhs, left_side=True, lower=True)

def upper_solve(factor, rhs):
    return lax.linalg.triangular_solve(factor, rhs, left_side=True, lower=True, transpose_a=True)

def reference(columns, pivots, start):
    highest = lax.Precision.HIGHEST
    gram = jnp.dot(columns.astype(jnp.float32), columns.T.astype(jnp.float32), precision=highest, preferred_element_type=jnp.float32) / VOX
    pivot_rows = jnp.take(columns, pivots, axis=1)
    core = jnp.dot(pivot_rows.astype(jnp.float32), pivot_rows.T.astype(jnp.float32), precision=highest, preferred_element_type=jnp.float32) / K
    core = core + core_shift * jnp.eye(K, dtype=jnp.float32)
    core_factor = jnp.linalg.cholesky(core)
    basis = start
    for step in range(ITERS):
        pushed = jnp.dot(gram.astype(jnp.float32), basis.astype(jnp.float32), precision=highest, preferred_element_type=jnp.float32)
        image = upper_solve(core_factor, lower_solve(core_factor, pushed))
        small = jnp.dot(image.T.astype(jnp.float32), jnp.dot(gram.astype(jnp.float32), image.astype(jnp.float32), precision=highest, preferred_element_type=jnp.float32).astype(jnp.float32), precision=highest, preferred_element_type=jnp.float32)
        small_factor = jnp.linalg.cholesky(small)
        basis = lower_solve(small_factor, image.T).T
    return jnp.dot(basis.T.astype(jnp.float32), columns.astype(jnp.float32), precision=highest, preferred_element_type=jnp.float32)
```

```python
import jax
import jax.numpy as jnp
from jax import lax
from jax.sharding import Mesh, PartitionSpec as P

ITERS = 3
CORE_SHIFT = 0.1
HIGHEST = lax.Precision.HIGHEST

FAR = ("z", "y")
NEAR = ("core", "panel")


def dot(a, b):
    return jnp.dot(a, b, precision=HIGHEST, preferred_element_type=jnp.float32)


def lower_solve(factor, rhs):
    return lax.linalg.triangular_solve(factor, rhs, left_side=True, lower=True)


def upper_solve(factor, rhs):
    return lax.linalg.triangular_solve(factor, rhs, left_side=True, lower=True, transpose_a=True)


def sum_everywhere(part):
    rows, width = part.shape
    far = lax.axis_size(FAR)
    near = lax.axis_size(NEAR)
    pieces = lax.all_to_all(part.reshape(far, rows // far, width), FAR, 0, 0, tiled=True)
    piece = jnp.sum(pieces, axis=0)
    copies = jnp.broadcast_to(piece[None], (near, rows // far, width))
    piece = jnp.sum(lax.all_to_all(copies, NEAR, 0, 0, tiled=True), axis=0)
    copies = jnp.broadcast_to(piece[None], (far, rows // far, width))
    return lax.all_to_all(copies, FAR, 0, 0, tiled=True).reshape(rows, width)


def body(columns, pivots, start):
    total_cols = columns.shape[0] * lax.axis_size("panel")
    width = columns.shape[1] // lax.axis_size("panel")
    place = lax.axis_index(("z", "y", "core", "panel"))
    voxels = width * lax.axis_size(("z", "y", "core", "panel"))
    cols = lax.all_to_all(columns, "panel", 1, 0, tiled=True)
    here = jnp.arange(width, dtype=jnp.int32) + place * width
    chosen = jnp.any(pivots[:, None] == here[None, :], axis=0).astype(jnp.float32)
    gram_part = dot(cols, cols.T)
    core_part = dot(cols * chosen[None, :], cols.T)
    both = sum_everywhere(jnp.concatenate([gram_part, core_part], axis=0))
    gram = both[:total_cols] / voxels
    core = both[total_cols:] / total_cols + CORE_SHIFT * jnp.eye(total_cols, dtype=jnp.float32)
    core_factor = jnp.linalg.cholesky(core)
    basis = start
    for step in range(ITERS):
        pushed = dot(gram, basis)
        image = upper_solve(core_factor, lower_solve(core_factor, pushed))
        small = dot(image.T, dot(gram, image))
        small_factor = jnp.linalg.cholesky(small)
        basis = lower_solve(small_factor, image.T).T
    return dot(basis.T, cols)


def solution(mesh):
    fine = Mesh(mesh.devices.reshape(8, 8, 2, 4), ("z", "y", "core", "panel"))
    rows = ("z", "y", "core")
    return jax.shard_map(
        body,
        mesh=fine,
        in_specs=(P("panel", rows), P(), P()),
        out_specs=P(None, rows + ("panel",)),
        check_vma=False,
    )
```

```python
import functools

import jax
import jax.numpy as jnp
from jax import lax
from jax.experimental import pallas as pl
from jax.experimental.pallas import tpu as pltpu
from jax.sharding import Mesh, PartitionSpec as P

ITERS = 3
CORE_SHIFT = 0.1
HIGHEST = lax.Precision.HIGHEST
SUB = 8
LANES = 128
BLOCK = 32

FAR = ("z", "y")
NEAR = ("core", "panel")
ROWS = ("z", "y", "core")


def dot(a, b, dims=(((1,), (0,)), ((), ()))):
    return lax.dot_general(a, b, dims, precision=HIGHEST, preferred_element_type=jnp.float32)


def inverse_factor(square, size):
    blocks = size // SUB
    row = lax.broadcasted_iota(jnp.int32, (SUB, LANES), 0)
    lane = lax.broadcasted_iota(jnp.int32, (SUB, LANES), 1)
    def spread(tile, r):
        return jnp.broadcast_to(tile[r : r + 1, :], (SUB, LANES))
    cols = [[None] * blocks for _ in range(size)]
    for j in range(size):
        for q in range(j // SUB, blocks):
            cols[j][q] = jnp.broadcast_to(square[SUB * q : SUB * q + SUB, j : j + 1], (SUB, LANES))
    inv = [[None] * blocks for _ in range(size)]
    roots = [jnp.zeros((SUB, LANES), jnp.float32) for _ in range(blocks)]
    for k in range(size):
        kq, kr = divmod(k, SUB)
        pivot = spread(cols[k][kq], kr)
        recip = 1.0 / pivot
        roots[kq] = jnp.where(row == kr, lax.rsqrt(pivot), roots[kq])
        lower = list(cols[k])
        lower[kq] = jnp.where(row > kr, cols[k][kq], 0.0)
        lower = [None if t is None else t * recip for t in lower]
        for j in range(k + 1, size):
            jq, jr = divmod(j, SUB)
            factor = spread(cols[k][jq], jr)
            for q in range(jq, blocks):
                cols[j][q] = cols[j][q] - lower[q] * factor
        inv[k][kq] = jnp.where(row == kr, 1.0, 0.0) - lower[kq]
        for q in range(kq + 1, blocks):
            inv[k][q] = -lower[q]
        for j in range(k):
            factor = spread(inv[j][kq], kr)
            for q in range(kq, blocks):
                inv[j][q] = inv[j][q] - lower[q] * factor
    out = []
    for q in range(blocks):
        tile = jnp.zeros((SUB, LANES), jnp.float32)
        for j in range(min(size, SUB * (q + 1))):
            tile = jnp.where(lane == j, inv[j][q], tile)
        out.append(tile * roots[q])
    return jnp.concatenate(out, axis=0)[:, :size]


def solve_kernel(voxels, both_ref, start_ref, cols_ref, out_ref, gram, work):
    size = cols_ref.shape[0]
    rank = start_ref.shape[1]
    every_row = lax.broadcasted_iota(jnp.int32, (size, size), 0)
    every_lane = lax.broadcasted_iota(jnp.int32, (size, size), 1)
    gram[...] = both_ref[:size, :] * (1.0 / voxels)
    work[...] = both_ref[size:, :] * (1.0 / size) + jnp.where(every_row == every_lane, CORE_SHIFT, 0.0)

    lane = lax.broadcasted_iota(jnp.int32, (BLOCK, size), 1)
    row = lax.broadcasted_iota(jnp.int32, (BLOCK, size), 0)

    def sweep(step, carry):
        base = step * BLOCK
        band = work[pl.ds(pl.multiple_of(base, BLOCK), BLOCK), :]
        factor = inverse_factor(pltpu.roll(band, size - base, axis=1)[:, :LANES], BLOCK)
        inside = (lane >= base) & (lane < base + BLOCK)
        band = jnp.where(inside, jnp.where(lane - base == row, -1.0, 0.0), band)
        scaled = dot(factor, band)
        outer = dot(scaled, scaled, (((0,), (0,)), ((), ())))
        keep_row = (every_row < base) | (every_row >= base + BLOCK)
        keep_lane = (every_lane < base) | (every_lane >= base + BLOCK)
        work[...] = jnp.where(keep_row & keep_lane, work[...], 0.0) - outer
        return carry

    lax.fori_loop(0, size // BLOCK, sweep, 0)

    def iterate(step, carry):
        image, _ = carry
        pushed = dot(gram[...], image)
        small = dot(image, pushed, (((0,), (0,)), ((), ())))
        small = jnp.concatenate([small, jnp.zeros((rank, LANES - rank), jnp.float32)], axis=1)
        factor = inverse_factor(small, rank)
        basis = dot(image, factor, (((1,), (1,)), ((), ())))
        return -dot(work[...], dot(pushed, factor, (((1,), (1,)), ((), ())))), basis

    image = -dot(work[...], dot(gram[...], start_ref[...]))
    _, basis = lax.fori_loop(0, ITERS, iterate, (image, image))
    out_ref[...] = dot(basis, cols_ref[...], (((0,), (0,)), ((), ())))


def solve(both, start, cols, voxels):
    size, width = cols.shape
    return pl.pallas_call(
        functools.partial(solve_kernel, voxels),
        out_shape=jax.ShapeDtypeStruct((start.shape[1], width), jnp.float32),
        in_specs=[pl.BlockSpec(memory_space=pltpu.VMEM)] * 3,
        out_specs=pl.BlockSpec(memory_space=pltpu.VMEM),
        scratch_shapes=[pltpu.VMEM((size, size), jnp.float32)] * 2,
        compiler_params=pltpu.CompilerParams(vmem_limit_bytes=32 * 2**20),
        name="solve",
    )(both, start, cols)


def sum_everywhere(part):
    rows, width = part.shape
    far = lax.axis_size(FAR)
    near = lax.axis_size(NEAR)
    pieces = lax.all_to_all(part.reshape(far, rows // far, width), FAR, 0, 0, tiled=True)
    piece = jnp.sum(pieces, axis=0)
    copies = jnp.broadcast_to(piece[None], (near, rows // far, width))
    piece = jnp.sum(lax.all_to_all(copies, NEAR, 0, 0, tiled=True), axis=0)
    copies = jnp.broadcast_to(piece[None], (far, rows // far, width))
    return lax.all_to_all(copies, FAR, 0, 0, tiled=True).reshape(rows, width)


def body(columns, pivots, start):
    width = columns.shape[1] // lax.axis_size("panel")
    place = lax.axis_index(ROWS + ("panel",))
    voxels = width * lax.axis_size(ROWS + ("panel",))
    cols = lax.all_to_all(columns, "panel", 1, 0, tiled=True)
    here = jnp.arange(width, dtype=jnp.int32) + place * width
    chosen = jnp.any(pivots[:, None] == here[None, :], axis=0).astype(jnp.float32)
    gram_part = dot(cols, cols.T)
    core_part = dot(cols * chosen[None, :], cols.T)
    both = sum_everywhere(jnp.concatenate([gram_part, core_part], axis=0))
    return solve(both, start, cols, voxels)


def solution(mesh):
    fine = Mesh(mesh.devices.reshape(8, 8, 2, 4), ROWS + ("panel",))
    return jax.shard_map(
        body,
        mesh=fine,
        in_specs=(P("panel", ROWS), P(), P()),
        out_specs=P(None, ROWS + ("panel",)),
        check_vma=False,
    )
```

```python
import functools

import jax
import jax.numpy as jnp
from jax import lax
from jax.experimental import pallas as pl
from jax.experimental.pallas import tpu as pltpu
from jax.sharding import Mesh, PartitionSpec as P

ITERS = 3
CORE_SHIFT = 0.1
HIGHEST = lax.Precision.HIGHEST
SUB = 8
LANES = 128
BLOCK = 32
SUBS = 2

FAR = ("z", "y")
NEAR = ("core", "panel")
ROWS = ("z", "y", "core")


def dot(a, b, dims=(((1,), (0,)), ((), ()))):
    return lax.dot_general(a, b, dims, precision=HIGHEST, preferred_element_type=jnp.float32)


def inverse_factor(square, size):
    blocks = size // SUB
    row = lax.broadcasted_iota(jnp.int32, (SUB, LANES), 0)
    lane = lax.broadcasted_iota(jnp.int32, (SUB, LANES), 1)
    def spread(tile, r):
        return jnp.broadcast_to(tile[r : r + 1, :], (SUB, LANES))
    cols = [[None] * blocks for _ in range(size)]
    for j in range(size):
        for q in range(j // SUB, blocks):
            cols[j][q] = jnp.broadcast_to(square[SUB * q : SUB * q + SUB, j : j + 1], (SUB, LANES))
    inv = [[None] * blocks for _ in range(size)]
    roots = [jnp.zeros((SUB, LANES), jnp.float32) for _ in range(blocks)]
    for k in range(size):
        kq, kr = divmod(k, SUB)
        pivot = spread(cols[k][kq], kr)
        recip = 1.0 / pivot
        roots[kq] = jnp.where(row == kr, lax.rsqrt(pivot), roots[kq])
        lower = list(cols[k])
        lower[kq] = jnp.where(row > kr, cols[k][kq], 0.0)
        lower = [None if t is None else t * recip for t in lower]
        for j in range(k + 1, size):
            jq, jr = divmod(j, SUB)
            factor = spread(cols[k][jq], jr)
            for q in range(jq, blocks):
                cols[j][q] = cols[j][q] - lower[q] * factor
        inv[k][kq] = jnp.where(row == kr, 1.0, 0.0) - lower[kq]
        for q in range(kq + 1, blocks):
            inv[k][q] = -lower[q]
        for j in range(k):
            factor = spread(inv[j][kq], kr)
            for q in range(kq, blocks):
                inv[j][q] = inv[j][q] - lower[q] * factor
    out = []
    for q in range(blocks):
        tile = jnp.zeros((SUB, LANES), jnp.float32)
        for j in range(min(size, SUB * (q + 1))):
            tile = jnp.where(lane == j, inv[j][q], tile)
        out.append(tile * roots[q])
    return jnp.concatenate(out, axis=0)[:, :size]


def pack_kernel(cols_ref, chosen_ref, out_ref):
    far, subs, width = out_ref.shape
    size = cols_ref.shape[0]
    each = size // far // subs
    cols = cols_ref[...]
    picked = cols * chosen_ref[...]
    both_lanes = (((1,), (1,)), ((), ()))
    gram = dot(cols, cols, both_lanes)
    core = dot(picked, cols, both_lanes)
    row = lax.broadcasted_iota(jnp.int32, (size, size), 0)
    lane = lax.broadcasted_iota(jnp.int32, (size, size), 1)
    packed = jnp.where(row >= lane, gram, core)
    diagonal = jnp.sum(jnp.where(row == lane, core, 0.0), axis=1, keepdims=True)
    spare = width - each * size
    spare_lane = lax.broadcasted_iota(jnp.int32, (far, spare), 1)
    for r in range(subs):
        tail = jnp.zeros((far, spare), jnp.float32)
        for h in range(each):
            first = (r * each + h) * far
            out_ref[:, r, h * size : (h + 1) * size] = packed[first : first + far, :]
            tail = jnp.where(spare_lane == h, diagonal[first : first + far, :], tail)
        out_ref[:, r, each * size :] = tail


def pack(cols, chosen, far):
    size = cols.shape[0]
    each = size // far // SUBS
    return pl.pallas_call(
        pack_kernel,
        out_shape=jax.ShapeDtypeStruct((far, SUBS, each * size + LANES), jnp.float32),
        in_specs=[pl.BlockSpec(memory_space=pltpu.VMEM)] * 2,
        out_specs=pl.BlockSpec(memory_space=pltpu.VMEM),
        compiler_params=pltpu.CompilerParams(vmem_limit_bytes=32 * 2**20),
        name="pack",
    )(cols, chosen)


def solve_kernel(voxels, packed_ref, start_ref, cols_ref, out_ref, gram, work):
    size = cols_ref.shape[0]
    rank = start_ref.shape[1]
    far, subs, width = packed_ref.shape
    each = size // far // subs
    every_row = lax.broadcasted_iota(jnp.int32, (size, size), 0)
    every_lane = lax.broadcasted_iota(jnp.int32, (size, size), 1)
    rows, diagonal = [], []
    for r in range(subs):
        tail = packed_ref[:, r, each * size :]
        for h in range(each):
            rows.append(packed_ref[:, r, h * size : (h + 1) * size])
            diagonal.append(tail[:, h : h + 1])
    packed = jnp.concatenate(rows, axis=0)
    flipped = packed.T
    gram[...] = jnp.where(every_row >= every_lane, packed, flipped) * (1.0 / voxels)
    core = jnp.where(every_row < every_lane, packed, flipped)
    core = jnp.where(every_row == every_lane, jnp.concatenate(diagonal, axis=0), core) * (1.0 / size)
    work[...] = core + jnp.where(every_row == every_lane, CORE_SHIFT, 0.0)

    lane = lax.broadcasted_iota(jnp.int32, (BLOCK, size), 1)
    row = lax.broadcasted_iota(jnp.int32, (BLOCK, size), 0)

    def sweep(step, carry):
        base = step * BLOCK
        band = work[pl.ds(pl.multiple_of(base, BLOCK), BLOCK), :]
        factor = inverse_factor(pltpu.roll(band, size - base, axis=1)[:, :LANES], BLOCK)
        inside = (lane >= base) & (lane < base + BLOCK)
        band = jnp.where(inside, jnp.where(lane - base == row, -1.0, 0.0), band)
        scaled = dot(factor, band)
        outer = dot(scaled, scaled, (((0,), (0,)), ((), ())))
        keep_row = (every_row < base) | (every_row >= base + BLOCK)
        keep_lane = (every_lane < base) | (every_lane >= base + BLOCK)
        work[...] = jnp.where(keep_row & keep_lane, work[...], 0.0) - outer
        return carry

    lax.fori_loop(0, size // BLOCK, sweep, 0)

    def iterate(step, carry):
        image, _ = carry
        pushed = dot(gram[...], image)
        small = dot(image, pushed, (((0,), (0,)), ((), ())))
        small = jnp.concatenate([small, jnp.zeros((rank, LANES - rank), jnp.float32)], axis=1)
        factor = inverse_factor(small, rank)
        basis = dot(image, factor, (((1,), (1,)), ((), ())))
        return -dot(work[...], dot(pushed, factor, (((1,), (1,)), ((), ())))), basis

    image = -dot(work[...], dot(gram[...], start_ref[...]))
    _, basis = lax.fori_loop(0, ITERS, iterate, (image, image))
    out_ref[...] = dot(basis, cols_ref[...], (((0,), (0,)), ((), ())))


def solve(packed, start, cols, voxels):
    size, width = cols.shape
    return pl.pallas_call(
        functools.partial(solve_kernel, voxels),
        out_shape=jax.ShapeDtypeStruct((start.shape[1], width), jnp.float32),
        in_specs=[pl.BlockSpec(memory_space=pltpu.VMEM)] * 3,
        out_specs=pl.BlockSpec(memory_space=pltpu.VMEM),
        scratch_shapes=[pltpu.VMEM((size, size), jnp.float32)] * 2,
        compiler_params=pltpu.CompilerParams(vmem_limit_bytes=32 * 2**20),
        name="solve",
    )(packed, start, cols)


def sum_everywhere(pieces):
    far, subs, width = pieces.shape
    near = lax.axis_size(NEAR)
    piece = jnp.sum(lax.all_to_all(pieces, FAR, 0, 0, tiled=True), axis=0)
    copies = jnp.broadcast_to(piece[None], (near, subs, width))
    piece = jnp.sum(lax.all_to_all(copies, NEAR, 0, 0, tiled=True), axis=0)
    copies = jnp.broadcast_to(piece[None], (far, subs, width))
    return lax.all_to_all(copies, FAR, 0, 0, tiled=True)


def body(columns, pivots, start):
    width = columns.shape[1] // lax.axis_size("panel")
    place = lax.axis_index(ROWS + ("panel",))
    voxels = width * lax.axis_size(ROWS + ("panel",))
    cols = lax.all_to_all(columns, "panel", 1, 0, tiled=True)
    here = jnp.arange(width, dtype=jnp.int32) + place * width
    chosen = jnp.any(pivots[:, None] == here[None, :], axis=0, keepdims=True).astype(jnp.float32)
    packed = sum_everywhere(pack(cols, chosen, lax.axis_size(FAR)))
    return solve(packed, start, cols, voxels)


def solution(mesh):
    fine = Mesh(mesh.devices.reshape(8, 8, 2, 4), ROWS + ("panel",))
    return jax.shard_map(
        body,
        mesh=fine,
        in_specs=(P("panel", ROWS), P(), P()),
        out_specs=P(None, ROWS + ("panel",)),
        check_vma=False,
    )
```

```python
import functools

import jax
import jax.numpy as jnp
from jax import lax
from jax.experimental import pallas as pl
from jax.experimental.pallas import tpu as pltpu
from jax.sharding import Mesh, PartitionSpec as P

ITERS = 3
CORE_SHIFT = 0.1
HIGHEST = lax.Precision.HIGHEST
SUB = 8
LANES = 128
BLOCK = 32
SUBS = 2

FAR = ("z", "y")
NEAR = ("core", "panel")
ROWS = ("z", "y", "core")


ROWS_BY_COLS = (((1,), (0,)), ((), ()))
ROWS_BY_ROWS = (((1,), (1,)), ((), ()))
COLS_BY_COLS = (((0,), (0,)), ((), ()))

LEFT = (0, 0, 1, 0, 2, 1)
RIGHT = (0, 1, 0, 2, 0, 1)


def dot(a, b, dims=ROWS_BY_COLS):
    return lax.dot_general(a, b, dims, precision=HIGHEST, preferred_element_type=jnp.float32)


def split(x):
    first = x.astype(jnp.bfloat16)
    rest = x - first.astype(jnp.float32)
    second = rest.astype(jnp.bfloat16)
    return first, second, (rest - second.astype(jnp.float32)).astype(jnp.bfloat16)


def stack_rows(x, order):
    parts = split(x)
    return jnp.concatenate([parts[i] for i in order], axis=0)


def by_parts(x, parts):
    n = x.shape[0]
    lhs = jnp.concatenate(split(x), axis=0)
    r0 = jnp.dot(lhs, parts[0], preferred_element_type=jnp.float32)
    r1 = jnp.dot(lhs[: 2 * n], parts[1], preferred_element_type=jnp.float32)
    r2 = jnp.dot(lhs[:n], parts[2], preferred_element_type=jnp.float32)
    return r0[:n] + ((r0[n : 2 * n] + r1[:n]) + (r0[2 * n :] + r1[n:] + r2))


def by_factor(factor, x):
    size = x.shape[0]
    first, second, third = [t.astype(jnp.float32) for t in split(factor)]
    group = lax.broadcasted_iota(jnp.int32, factor.shape, 1) // size
    left = jnp.where(group == 2, second, first)
    right = jnp.where(group == 0, third, second)
    lhs = jnp.concatenate([left, right[:, : 2 * size]], axis=1).astype(jnp.bfloat16)
    return jnp.dot(lhs, stack_rows(x, RIGHT), preferred_element_type=jnp.float32)


def outer_square(x):
    return lax.dot_general(
        stack_rows(x, LEFT), stack_rows(x, RIGHT), COLS_BY_COLS, preferred_element_type=jnp.float32
    )


def inverse_factor(square, size):
    blocks = size // SUB
    row = lax.broadcasted_iota(jnp.int32, (SUB, LANES), 0)
    lane = lax.broadcasted_iota(jnp.int32, (SUB, LANES), 1)

    def spread(tile, r):
        return jnp.broadcast_to(tile[r : r + 1, :], (SUB, LANES))

    cols = [[None] * blocks for _ in range(size)]
    for j in range(size):
        for q in range(j // SUB, blocks):
            cols[j][q] = jnp.broadcast_to(square[SUB * q : SUB * q + SUB, j : j + 1], (SUB, LANES))
    inv = [jnp.where(lane % size == row + SUB * q, 1.0, 0.0) for q in range(blocks)]
    pivots = [jnp.zeros((SUB, LANES), jnp.float32) for _ in range(blocks)]
    for k in range(size):
        kq, kr = divmod(k, SUB)
        pivot = spread(cols[k][kq], kr)
        recip = pl.reciprocal(pivot, approx=True)
        recip = recip * (2.0 - pivot * recip)
        pivots[kq] = jnp.where(row == kr, pivot, pivots[kq])
        lower = list(cols[k])
        lower[kq] = jnp.where(row > kr, cols[k][kq], 0.0)
        lower = [None if t is None else t * recip for t in lower]
        for j in range(k + 1, size):
            jq, jr = divmod(j, SUB)
            factor = spread(cols[k][jq], jr)
            for q in range(jq, blocks):
                cols[j][q] = cols[j][q] - lower[q] * factor
        above = spread(inv[kq], kr)
        for q in range(kq, blocks):
            inv[q] = inv[q] - lower[q] * above
    return jnp.concatenate([t * lax.rsqrt(p) for t, p in zip(inv, pivots)], axis=0)


def pack_kernel(cols_ref, chosen_ref, out_ref):
    far, subs, width = out_ref.shape
    size = cols_ref.shape[0]
    each = size // far // subs
    cols = cols_ref[...]
    picked = cols * chosen_ref[...]
    gram = dot(cols, cols, ROWS_BY_ROWS)
    core = dot(picked, cols, ROWS_BY_ROWS)
    row = lax.broadcasted_iota(jnp.int32, (size, size), 0)
    lane = lax.broadcasted_iota(jnp.int32, (size, size), 1)
    packed = jnp.where(row >= lane, gram, core)
    diagonal = jnp.sum(jnp.where(row == lane, core, 0.0), axis=1, keepdims=True)
    spare = width - each * size
    spare_lane = lax.broadcasted_iota(jnp.int32, (far, spare), 1)
    for r in range(subs):
        tail = jnp.zeros((far, spare), jnp.float32)
        for h in range(each):
            first = (r * each + h) * far
            out_ref[:, r, h * size : (h + 1) * size] = packed[first : first + far, :]
            tail = jnp.where(spare_lane == h, diagonal[first : first + far, :], tail)
        out_ref[:, r, each * size :] = tail


def pack(cols, chosen, far):
    size = cols.shape[0]
    each = size // far // SUBS
    return pl.pallas_call(
        pack_kernel,
        out_shape=jax.ShapeDtypeStruct((far, SUBS, each * size + LANES), jnp.float32),
        in_specs=[pl.BlockSpec(memory_space=pltpu.VMEM)] * 2,
        out_specs=pl.BlockSpec(memory_space=pltpu.VMEM),
        compiler_params=pltpu.CompilerParams(vmem_limit_bytes=32 * 2**20),
        name="pack",
    )(cols, chosen)


def solve_kernel(voxels, packed_ref, start_ref, cols_ref, out_ref, work, basis, gram_parts, inverse_parts):
    size = cols_ref.shape[0]
    rank = start_ref.shape[0]
    far, subs, width = packed_ref.shape
    each = size // far // subs
    every_row = lax.broadcasted_iota(jnp.int32, (size, size), 0)
    every_lane = lax.broadcasted_iota(jnp.int32, (size, size), 1)
    rows, diagonal = [], []
    for r in range(subs):
        tail = packed_ref[:, r, each * size :]
        for h in range(each):
            rows.append(packed_ref[:, r, h * size : (h + 1) * size])
            diagonal.append(tail[:, h : h + 1])
    packed = jnp.concatenate(rows, axis=0)
    flipped = packed.T
    for i, part in enumerate(split(jnp.where(every_row >= every_lane, packed, flipped) * (1.0 / voxels))):
        gram_parts[i] = part
    core = jnp.where(every_row < every_lane, packed, flipped)
    core = jnp.where(every_row == every_lane, jnp.concatenate(diagonal, axis=0), core) * (1.0 / size)
    core = core + jnp.where(every_row == every_lane, CORE_SHIFT, 0.0)
    work[...] = core

    lane = lax.broadcasted_iota(jnp.int32, (BLOCK, size), 1)
    row = lax.broadcasted_iota(jnp.int32, (BLOCK, size), 0)

    def update(scaled, base):
        keep_row = (every_row < base) | (every_row >= base + BLOCK)
        keep_lane = (every_lane < base) | (every_lane >= base + BLOCK)
        work[...] = jnp.where(keep_row & keep_lane, work[...], 0.0) - outer_square(scaled)

    def sweep(step, carry):
        scaled, corner = carry
        base = step * BLOCK
        factor = inverse_factor(corner, BLOCK)
        update(scaled, base - BLOCK)
        band = work[pl.ds(pl.multiple_of(base, BLOCK), BLOCK), :]
        inside = (lane >= base) & (lane < base + BLOCK)
        band = jnp.where(inside, jnp.where(lane - base == row, -1.0, 0.0), band)
        scaled = by_factor(factor, band)
        then = jnp.minimum(base + BLOCK, size - BLOCK)
        tile = pl.multiple_of(then // LANES * LANES, LANES)
        corner = work[pl.ds(pl.multiple_of(then, BLOCK), BLOCK), pl.ds(tile, LANES)]
        own = scaled[:, :LANES]
        for t in range(LANES, size, LANES):
            own = jnp.where(then >= t, scaled[:, t : t + LANES], own)
        shift = LANES - lax.rem(then, LANES)
        own = pltpu.roll(own, shift, axis=1)
        corner = pltpu.roll(corner, shift, axis=1) - outer_square(own)[:BLOCK, :]
        return scaled, corner

    nothing = jnp.zeros((BLOCK, size), jnp.float32)
    scaled, _ = lax.fori_loop(0, size // BLOCK, sweep, (nothing, core[:BLOCK, :LANES]))
    update(scaled, size - BLOCK)
    for i, part in enumerate(split(-work[...])):
        inverse_parts[i] = part

    def by(ref, x):
        return by_parts(x, (ref[0], ref[1], ref[2]))

    def iterate(step, carry):
        image, pushed = carry
        small = dot(image, pushed, ROWS_BY_ROWS)
        small = jnp.concatenate([small, jnp.zeros((rank, LANES - rank), jnp.float32)], axis=1)
        factor = inverse_factor(small, rank)
        top = jnp.max(jnp.max(jnp.abs(pushed), axis=0, keepdims=True), axis=1, keepdims=True)
        ahead = by(inverse_parts, pushed * (1.0 / top))
        ahead_pushed = by(gram_parts, ahead)
        basis[...] = by_factor(factor, image)
        scaled_factor = factor * top
        return by_factor(scaled_factor, ahead), by_factor(scaled_factor, ahead_pushed)

    image = by(inverse_parts, by(gram_parts, start_ref[...]))
    lax.fori_loop(0, ITERS, iterate, (image, by(gram_parts, image)))
    out_ref[...] = dot(basis[...], cols_ref[...])


def solve(packed, start, cols, voxels):
    size, width = cols.shape
    return pl.pallas_call(
        functools.partial(solve_kernel, voxels),
        out_shape=jax.ShapeDtypeStruct((start.shape[0], width), jnp.float32),
        in_specs=[pl.BlockSpec(memory_space=pltpu.VMEM)] * 3,
        out_specs=pl.BlockSpec(memory_space=pltpu.VMEM),
        scratch_shapes=[
            pltpu.VMEM((size, size), jnp.float32),
            pltpu.VMEM(start.shape, jnp.float32),
            pltpu.VMEM((3, size, size), jnp.bfloat16),
            pltpu.VMEM((3, size, size), jnp.bfloat16),
        ],
        compiler_params=pltpu.CompilerParams(vmem_limit_bytes=32 * 2**20),
        name="solve",
    )(packed, start, cols)


def sum_everywhere(pieces):
    far, subs, width = pieces.shape
    near = lax.axis_size(NEAR)
    piece = jnp.sum(lax.all_to_all(pieces, FAR, 0, 0, tiled=True), axis=0)
    copies = jnp.broadcast_to(piece[None], (near, subs, width))
    piece = jnp.sum(lax.all_to_all(copies, NEAR, 0, 0, tiled=True), axis=0)
    copies = jnp.broadcast_to(piece[None], (far, subs, width))
    return lax.all_to_all(copies, FAR, 0, 0, tiled=True)


def body(columns, pivots, start):
    width = columns.shape[1] // lax.axis_size("panel")
    place = lax.axis_index(ROWS + ("panel",))
    voxels = width * lax.axis_size(ROWS + ("panel",))
    cols = lax.all_to_all(columns, "panel", 1, 0, tiled=True)
    here = jnp.arange(width, dtype=jnp.int32) + place * width
    chosen = jnp.any(pivots[:, None] == here[None, :], axis=0, keepdims=True).astype(jnp.float32)
    packed = sum_everywhere(pack(cols, chosen, lax.axis_size(FAR)))
    return solve(packed, start.T, cols, voxels)


def solution(mesh):
    fine = Mesh(mesh.devices.reshape(8, 8, 2, 4), ROWS + ("panel",))
    return jax.shard_map(
        body,
        mesh=fine,
        in_specs=(P("panel", ROWS), P(), P()),
        out_specs=P(None, ROWS + ("panel",)),
        check_vma=False,
    )
```

```python
import functools

import jax
import jax.numpy as jnp
from jax import lax
from jax.experimental import pallas as pl
from jax.experimental.pallas import tpu as pltpu
from jax.sharding import Mesh, PartitionSpec as P

ITERS = 3
CORE_SHIFT = 0.1
HIGHEST = lax.Precision.HIGHEST
SUB = 8
LANES = 128
BLOCK = 32
PANEL = 16
SUBS = 4

FAR = ("panel", "y")
NEAR = ("z", "core")
ROWS = ("z", "y", "core")


ROWS_BY_COLS = (((1,), (0,)), ((), ()))
ROWS_BY_ROWS = (((1,), (1,)), ((), ()))
COLS_BY_COLS = (((0,), (0,)), ((), ()))

LEFT = (0, 0, 1, 0, 2, 1)
RIGHT = (0, 1, 0, 2, 0, 1)


def dot(a, b, dims=ROWS_BY_COLS):
    return lax.dot_general(a, b, dims, precision=HIGHEST, preferred_element_type=jnp.float32)


def split(x):
    first = x.astype(jnp.bfloat16)
    rest = x - first.astype(jnp.float32)
    second = rest.astype(jnp.bfloat16)
    return first, second, (rest - second.astype(jnp.float32)).astype(jnp.bfloat16)


def stack_rows(x, order):
    parts = split(x)
    return jnp.concatenate([parts[i] for i in order], axis=0)


def by_parts(x, parts):
    n = x.shape[0]
    lhs = jnp.concatenate(split(x), axis=0)
    r0 = jnp.dot(lhs, parts[0], preferred_element_type=jnp.float32)
    r1 = jnp.dot(lhs[: 2 * n], parts[1], preferred_element_type=jnp.float32)
    r2 = jnp.dot(lhs[:n], parts[2], preferred_element_type=jnp.float32)
    return r0[:n] + ((r0[n : 2 * n] + r1[:n]) + (r0[2 * n :] + r1[n:] + r2))


def by_factor(factor, x):
    size = x.shape[0]
    first, second, third = [t.astype(jnp.float32) for t in split(factor)]
    group = lax.broadcasted_iota(jnp.int32, factor.shape, 1) // size
    left = jnp.where(group == 0, 0.0, jnp.where(group == 3, second, first))
    right = jnp.where(group == 0, 0.0, jnp.where(group == 3, second, jnp.where(group == 2, third, first)))
    lhs = jnp.concatenate([left, right], axis=1).astype(jnp.bfloat16)
    return jnp.dot(lhs, stack_rows(x, (0, 0, 1, 0, 0, 2, 0, 1)), preferred_element_type=jnp.float32)


def by_columns(x, y):
    return lax.dot_general(
        stack_rows(x, LEFT), stack_rows(y, RIGHT), COLS_BY_COLS, preferred_element_type=jnp.float32
    )


def inverse_factor(square, size):
    blocks = size // SUB
    row = lax.broadcasted_iota(jnp.int32, (SUB, LANES), 0)
    lane = lax.broadcasted_iota(jnp.int32, (SUB, LANES), 1)

    def spread(tile, r):
        return jnp.broadcast_to(tile[r : r + 1, :], (SUB, LANES))

    rows = []
    for q in range(blocks):
        unit = jnp.where(lane % size == row + SUB * q, 1.0, 0.0)
        rows.append(jnp.where(lane < size, square[SUB * q : SUB * q + SUB, :], unit))
    pivots = [jnp.zeros((SUB, LANES), jnp.float32) for _ in range(blocks)]
    for first in range(0, size, PANEL):
        last = first + PANEL - 1
        cols = {}
        for j in range(first, last + 1):
            for q in range(j // SUB, blocks):
                cols[j, q] = jnp.broadcast_to(rows[q][:, j : j + 1], (SUB, LANES))
        pivot = spread(cols[first, first // SUB], first % SUB)
        for k in range(first, last + 1):
            kq, kr = divmod(k, SUB)
            rough = pl.reciprocal(pivot, approx=True)
            fix = 2.0 - pivot * rough
            recip = rough * fix
            pivots[kq] = jnp.where(row == kr, pivot, pivots[kq])
            if k < last:
                nq, nr = divmod(k + 1, SUB)
                beside = spread(cols[k, nq], nr)
                pivot = spread(cols[k + 1, nq], nr) - (beside * beside * rough) * fix
            lower = {q: cols[k, q] for q in range(kq, blocks)}
            lower[kq] = jnp.where(row > kr, lower[kq], 0.0)
            lower = {q: t * recip for q, t in lower.items()}
            for j in range(k + 1, last + 1):
                jq, jr = divmod(j, SUB)
                factor = spread(cols[k, jq], jr)
                for q in range(jq, blocks):
                    cols[j, q] = cols[j, q] - lower[q] * factor
            above = spread(rows[kq], kr)
            for q in range(kq, blocks):
                rows[q] = rows[q] - lower[q] * above
    return jnp.concatenate([t * lax.rsqrt(p) for t, p in zip(rows, pivots)], axis=0)


def pack_kernel(cols_ref, chosen_ref, out_ref):
    far, subs, width = out_ref.shape
    size = cols_ref.shape[0]
    each = size // far // subs
    row = lax.broadcasted_iota(jnp.int32, (size, size), 0)
    lane = lax.broadcasted_iota(jnp.int32, (size, size), 1)
    high, middle, low = split(cols_ref[...])
    chosen = chosen_ref[...].astype(jnp.bfloat16)
    first = jnp.concatenate([high, high * chosen], axis=0)
    second = jnp.concatenate([middle, middle * chosen], axis=0)

    def product(x, y):
        return lax.dot_general(x, y, ROWS_BY_ROWS, preferred_element_type=jnp.float32)

    mirrored = product(first, low) + product(first, middle)
    plain = product(second, middle) + product(first, high)
    gram_half, core_half = mirrored[:size], mirrored[size:]
    turned = jnp.where(row <= lane, gram_half, core_half).T
    packed = jnp.where(row >= lane, plain[:size] + gram_half, plain[size:] + core_half) + turned
    core_diagonal = plain[size:] + 2.0 * core_half
    diagonal = jnp.sum(jnp.where(row == lane, core_diagonal, 0.0), axis=1, keepdims=True)
    spare = width - each * size
    spare_lane = lax.broadcasted_iota(jnp.int32, (far, spare), 1)
    for r in range(subs):
        tail = jnp.zeros((far, spare), jnp.float32)
        for h in range(each):
            at = (r * each + h) * far
            out_ref[:, r, h * size : (h + 1) * size] = packed[at : at + far, :]
            tail = jnp.where(spare_lane == h, diagonal[at : at + far, :], tail)
        out_ref[:, r, each * size :] = tail


def pack(cols, chosen, far):
    size = cols.shape[0]
    each = size // far // SUBS
    return pl.pallas_call(
        pack_kernel,
        out_shape=jax.ShapeDtypeStruct((far, SUBS, each * size + LANES), jnp.float32),
        in_specs=[pl.BlockSpec(memory_space=pltpu.VMEM)] * 2,
        out_specs=pl.BlockSpec(memory_space=pltpu.VMEM),
        compiler_params=pltpu.CompilerParams(vmem_limit_bytes=32 * 2**20),
        name="pack",
    )(cols, chosen)


def solve_kernel(voxels, packed_ref, start_ref, cols_ref, out_ref, work, gram, basis, gram_parts, inverse_parts, cols_parts):
    size = cols_ref.shape[0]
    rank = start_ref.shape[0]
    far, subs, width = packed_ref.shape
    each = size // far // subs
    every_row = lax.broadcasted_iota(jnp.int32, (size, size), 0)
    every_lane = lax.broadcasted_iota(jnp.int32, (size, size), 1)
    rows, diagonal = [], []
    for r in range(subs):
        tail = packed_ref[:, r, each * size :]
        for h in range(each):
            rows.append(packed_ref[:, r, h * size : (h + 1) * size])
            diagonal.append(tail[:, h : h + 1])
    packed = jnp.concatenate(rows, axis=0)
    flipped = packed.T
    gram[...] = jnp.where(every_row >= every_lane, packed, flipped) * (1.0 / voxels)
    core = jnp.where(every_row < every_lane, packed, flipped)
    core = jnp.where(every_row == every_lane, jnp.concatenate(diagonal, axis=0), core) * (1.0 / size)
    core = core + jnp.where(every_row == every_lane, CORE_SHIFT, 0.0)
    work[...] = core

    lane = lax.broadcasted_iota(jnp.int32, (BLOCK, size), 1)
    row = lax.broadcasted_iota(jnp.int32, (BLOCK, size), 0)

    def update(scaled, base):
        keep_row = (every_row < base) | (every_row >= base + BLOCK)
        keep_lane = (every_lane < base) | (every_lane >= base + BLOCK)
        work[...] = jnp.where(keep_row & keep_lane, work[...], 0.0) - by_columns(scaled, scaled)

    def sweep(step, carry):
        scaled, corner = carry
        base = pl.multiple_of(step * BLOCK, BLOCK)
        rows_here = pl.ds(base, BLOCK)
        factor = inverse_factor(corner, BLOCK)
        update(scaled, base - BLOCK)
        band = work[rows_here, :]
        inside = (lane >= base) & (lane < base + BLOCK)
        band = jnp.where(inside, jnp.where(lane - base == row, -1.0, 0.0), band)
        then = jnp.minimum(base + BLOCK, size - BLOCK)
        tile = pl.multiple_of(then // LANES * LANES, LANES)
        shift = LANES - lax.rem(then, LANES)
        own = band[:, :LANES]
        for t in range(LANES, size, LANES):
            own = jnp.where(then >= t, band[:, t : t + LANES], own)
        own = pltpu.roll(own, shift, axis=1)
        corner = pltpu.roll(work[pl.ds(pl.multiple_of(then, BLOCK), BLOCK), pl.ds(tile, LANES)], shift, axis=1)
        own = by_factor(factor, own)
        corner = corner - by_columns(own, own)[:BLOCK, :]
        scaled = by_factor(factor, band)
        for i, part in enumerate(split(cols_ref[rows_here, :])):
            cols_parts[i, rows_here, :] = part
        for i, part in enumerate(split(gram[rows_here, :])):
            gram_parts[i, rows_here, :] = part
        return scaled, corner

    nothing = jnp.zeros((BLOCK, size), jnp.float32)
    scaled, _ = lax.fori_loop(0, size // BLOCK, sweep, (nothing, core[:BLOCK, :LANES]))
    update(scaled, size - BLOCK)
    for i, part in enumerate(split(-work[...])):
        inverse_parts[i] = part

    def by(ref, x):
        return by_parts(x, (ref[0], ref[1], ref[2]))

    def iterate(step, carry):
        image, pushed = carry
        small = dot(image, pushed, ROWS_BY_ROWS)
        small = jnp.concatenate([small, jnp.zeros((rank, LANES - rank), jnp.float32)], axis=1)
        factor = inverse_factor(small, rank)
        top = jnp.max(jnp.max(jnp.abs(pushed), axis=0, keepdims=True), axis=1, keepdims=True)
        ahead = by(inverse_parts, pushed * (1.0 / top))
        ahead_pushed = by(gram_parts, ahead)
        basis[...] = by_factor(factor, image)
        scaled_factor = factor * top
        return by_factor(scaled_factor, ahead), by_factor(scaled_factor, ahead_pushed)

    image = by(inverse_parts, by(gram_parts, start_ref[...]))
    lax.fori_loop(0, ITERS, iterate, (image, by(gram_parts, image)))
    out_ref[...] = by(cols_parts, basis[...])


def solve(packed, start, cols, voxels):
    size, width = cols.shape
    rank = start.shape[0]
    return pl.pallas_call(
        functools.partial(solve_kernel, voxels),
        out_shape=jax.ShapeDtypeStruct((rank, width), jnp.float32),
        in_specs=[pl.BlockSpec(memory_space=pltpu.VMEM)] * 3,
        out_specs=pl.BlockSpec(memory_space=pltpu.VMEM),
        scratch_shapes=[
            pltpu.VMEM((size, size), jnp.float32),
            pltpu.VMEM((size, size), jnp.float32),
            pltpu.VMEM((rank, size), jnp.float32),
            pltpu.VMEM((3, size, size), jnp.bfloat16),
            pltpu.VMEM((3, size, size), jnp.bfloat16),
            pltpu.VMEM((3, size, width), jnp.bfloat16),
        ],
        compiler_params=pltpu.CompilerParams(vmem_limit_bytes=32 * 2**20),
        name="solve",
    )(packed, start, cols)


def sum_everywhere(pieces):
    far, subs, width = pieces.shape
    near = lax.axis_size(NEAR)
    piece = jnp.sum(lax.all_to_all(pieces, FAR, 0, 0, tiled=True), axis=0)
    copies = jnp.broadcast_to(piece[None], (near, subs, width))
    piece = jnp.sum(lax.all_to_all(copies, NEAR, 0, 0, tiled=True), axis=0)
    copies = jnp.broadcast_to(piece[None], (far, subs, width))
    return lax.all_to_all(copies, FAR, 0, 0, tiled=True)


def body(columns, pivots, start):
    width = columns.shape[1] // lax.axis_size("panel")
    place = lax.axis_index(ROWS + ("panel",))
    voxels = width * lax.axis_size(ROWS + ("panel",))
    cols = lax.all_to_all(columns, "panel", 1, 0, tiled=True)
    here = jnp.arange(width, dtype=jnp.int32) + place * width
    chosen = jnp.any(pivots[:, None] == here[None, :], axis=0, keepdims=True).astype(jnp.float32)
    packed = sum_everywhere(pack(cols, chosen, lax.axis_size(FAR)))
    return solve(packed, start.T, cols, voxels)


def solution(mesh):
    fine = Mesh(mesh.devices.reshape(8, 8, 2, 4), ROWS + ("panel",))
    return jax.shard_map(
        body,
        mesh=fine,
        in_specs=(P("panel", ROWS), P(), P()),
        out_specs=P(None, ROWS + ("panel",)),
        check_vma=False,
    )
```

```python
import functools

import jax
import jax.numpy as jnp
from jax import lax
from jax.experimental import pallas as pl
from jax.experimental.pallas import tpu as pltpu
from jax.sharding import Mesh, PartitionSpec as P

ITERS = 3
CORE_SHIFT = 0.1
HIGHEST = lax.Precision.HIGHEST
SUB = 8
LANES = 128
BLOCK = 32
PANEL = 16
SUBS = 4

FAR = ("panel", "y")
NEAR = ("z", "core")
ROWS = ("z", "y", "core")


ROWS_BY_COLS = (((1,), (0,)), ((), ()))
ROWS_BY_ROWS = (((1,), (1,)), ((), ()))
COLS_BY_COLS = (((0,), (0,)), ((), ()))

LEFT = (0, 0, 1, 0, 2, 1)
RIGHT = (0, 1, 0, 2, 0, 1)


def dot(a, b, dims=ROWS_BY_COLS):
    return lax.dot_general(a, b, dims, precision=HIGHEST, preferred_element_type=jnp.float32)


def split(x):
    first = x.astype(jnp.bfloat16)
    rest = x - first.astype(jnp.float32)
    second = rest.astype(jnp.bfloat16)
    return first, second, (rest - second.astype(jnp.float32)).astype(jnp.bfloat16)


def stack_rows(x, order):
    parts = split(x)
    return jnp.concatenate([parts[i] for i in order], axis=0)


def by_parts(x, parts):
    n = x.shape[0]
    lhs = jnp.concatenate(split(x), axis=0)
    r0 = jnp.dot(lhs, parts[0], preferred_element_type=jnp.float32)
    r1 = jnp.dot(lhs[: 2 * n], parts[1], preferred_element_type=jnp.float32)
    r2 = jnp.dot(lhs[:n], parts[2], preferred_element_type=jnp.float32)
    return r0[:n] + ((r0[n : 2 * n] + r1[:n]) + (r0[2 * n :] + r1[n:] + r2))


def by_factor(factor, x):
    size = x.shape[0]
    first, second, third = [t.astype(jnp.float32) for t in split(factor)]
    group = lax.broadcasted_iota(jnp.int32, factor.shape, 1) // size
    left = jnp.where(group == 0, 0.0, jnp.where(group == 3, second, first))
    right = jnp.where(group == 0, 0.0, jnp.where(group == 3, second, jnp.where(group == 2, third, first)))
    lhs = jnp.concatenate([left, right], axis=1).astype(jnp.bfloat16)
    return jnp.dot(lhs, stack_rows(x, (0, 0, 1, 0, 0, 2, 0, 1)), preferred_element_type=jnp.float32)


def by_columns(x, y):
    return lax.dot_general(
        stack_rows(x, LEFT), stack_rows(y, RIGHT), COLS_BY_COLS, preferred_element_type=jnp.float32
    )


def inverse_factor(square, size):
    blocks = size // SUB
    row = lax.broadcasted_iota(jnp.int32, (SUB, LANES), 0)
    lane = lax.broadcasted_iota(jnp.int32, (SUB, LANES), 1)

    def spread(tile, r):
        return jnp.broadcast_to(tile[r : r + 1, :], (SUB, LANES))

    rows = []
    for q in range(blocks):
        unit = jnp.where(lane % size == row + SUB * q, 1.0, 0.0)
        rows.append(jnp.where(lane < size, square[SUB * q : SUB * q + SUB, :], unit))
    pivots = [jnp.zeros((SUB, LANES), jnp.float32) for _ in range(blocks)]
    for first in range(0, size, PANEL):
        last = first + PANEL - 1
        cols = {}
        for j in range(first, last + 1):
            for q in range(j // SUB, blocks):
                cols[j, q] = jnp.broadcast_to(rows[q][:, j : j + 1], (SUB, LANES))
        pivot = spread(cols[first, first // SUB], first % SUB)
        for k in range(first, last + 1):
            kq, kr = divmod(k, SUB)
            rough = pl.reciprocal(pivot, approx=True)
            fix = 2.0 - pivot * rough
            recip = rough * fix
            pivots[kq] = jnp.where(row == kr, pivot, pivots[kq])
            if k < last:
                nq, nr = divmod(k + 1, SUB)
                beside = spread(cols[k, nq], nr)
                pivot = spread(cols[k + 1, nq], nr) - (beside * beside * rough) * fix
            lower = {q: cols[k, q] for q in range(kq, blocks)}
            lower[kq] = jnp.where(row > kr, lower[kq], 0.0)
            lower = {q: t * recip for q, t in lower.items()}
            for j in range(k + 1, last + 1):
                jq, jr = divmod(j, SUB)
                factor = spread(cols[k, jq], jr)
                for q in range(jq, blocks):
                    cols[j, q] = cols[j, q] - lower[q] * factor
            above = spread(rows[kq], kr)
            for q in range(kq, blocks):
                rows[q] = rows[q] - lower[q] * above
    return jnp.concatenate([t * lax.rsqrt(p) for t, p in zip(rows, pivots)], axis=0)


def chosen_here(pivots_ref, width):
    place = lax.axis_index(ROWS + ("panel",))
    lane = lax.broadcasted_iota(jnp.int32, (LANES, LANES), 1).astype(jnp.float32)
    chosen = []
    for first in range(0, width, LANES):
        chosen.append(jnp.zeros((LANES, LANES), jnp.float32))
    for group in range(pivots_ref.shape[0]):
        here = (pivots_ref[group : group + 1, :] - place * width).astype(jnp.float32)
        here = jnp.broadcast_to(here, (LANES, LANES)).T
        for i in range(len(chosen)):
            chosen[i] = jnp.where(here == lane + float(i * LANES), 1.0, chosen[i])
    return jnp.concatenate([jnp.max(c, axis=0, keepdims=True) for c in chosen], axis=1)


def pack_kernel(cols_ref, pivots_ref, out_ref):
    far, subs, width = out_ref.shape
    size = cols_ref.shape[0]
    each = size // far // subs
    row = lax.broadcasted_iota(jnp.int32, (size, size), 0)
    lane = lax.broadcasted_iota(jnp.int32, (size, size), 1)
    high, middle, low = split(cols_ref[...])
    chosen = chosen_here(pivots_ref, cols_ref.shape[1]).astype(jnp.bfloat16)
    first = jnp.concatenate([high, high * chosen], axis=0)
    second = jnp.concatenate([middle, middle * chosen], axis=0)

    def product(x, y):
        return lax.dot_general(x, y, ROWS_BY_ROWS, preferred_element_type=jnp.float32)

    mirrored = product(first, low) + product(first, middle)
    plain = product(second, middle) + product(first, high)
    gram_half, core_half = mirrored[:size], mirrored[size:]
    turned = jnp.where(row <= lane, gram_half, core_half).T
    packed = jnp.where(row >= lane, plain[:size] + gram_half, plain[size:] + core_half) + turned
    core_diagonal = plain[size:] + 2.0 * core_half
    diagonal = jnp.sum(jnp.where(row == lane, core_diagonal, 0.0), axis=1, keepdims=True)
    spare = width - each * size
    spare_lane = lax.broadcasted_iota(jnp.int32, (far, spare), 1)
    for r in range(subs):
        tail = jnp.zeros((far, spare), jnp.float32)
        for h in range(each):
            at = (r * each + h) * far
            out_ref[:, r, h * size : (h + 1) * size] = packed[at : at + far, :]
            tail = jnp.where(spare_lane == h, diagonal[at : at + far, :], tail)
        out_ref[:, r, each * size :] = tail


def pack(cols, pivots, far):
    size = cols.shape[0]
    each = size // far // SUBS
    return pl.pallas_call(
        pack_kernel,
        out_shape=jax.ShapeDtypeStruct((far, SUBS, each * size + LANES), jnp.float32),
        in_specs=[pl.BlockSpec(memory_space=pltpu.VMEM)] * 2,
        out_specs=pl.BlockSpec(memory_space=pltpu.VMEM),
        compiler_params=pltpu.CompilerParams(vmem_limit_bytes=32 * 2**20),
        name="pack",
    )(cols, pivots.reshape(-1, LANES))


def solve_kernel(voxels, packed_ref, start_ref, cols_ref, out_ref, work, gram, basis, gram_parts, inverse_parts, cols_parts):
    size = cols_ref.shape[0]
    rank = start_ref.shape[0]
    far, subs, width = packed_ref.shape
    each = size // far // subs
    every_row = lax.broadcasted_iota(jnp.int32, (size, size), 0)
    every_lane = lax.broadcasted_iota(jnp.int32, (size, size), 1)
    rows, diagonal = [], []
    for r in range(subs):
        tail = packed_ref[:, r, each * size :]
        for h in range(each):
            rows.append(packed_ref[:, r, h * size : (h + 1) * size])
            diagonal.append(tail[:, h : h + 1])
    packed = jnp.concatenate(rows, axis=0)
    flipped = packed.T
    gram[...] = jnp.where(every_row >= every_lane, packed, flipped) * (1.0 / voxels)
    core = jnp.where(every_row < every_lane, packed, flipped)
    core = jnp.where(every_row == every_lane, jnp.concatenate(diagonal, axis=0), core) * (1.0 / size)
    core = core + jnp.where(every_row == every_lane, CORE_SHIFT, 0.0)
    work[...] = core

    lane = lax.broadcasted_iota(jnp.int32, (BLOCK, size), 1)
    row = lax.broadcasted_iota(jnp.int32, (BLOCK, size), 0)

    def update(scaled, base):
        keep_row = (every_row < base) | (every_row >= base + BLOCK)
        keep_lane = (every_lane < base) | (every_lane >= base + BLOCK)
        work[...] = jnp.where(keep_row & keep_lane, work[...], 0.0) - by_columns(scaled, scaled)

    def sweep(step, carry):
        scaled, corner = carry
        base = pl.multiple_of(step * BLOCK, BLOCK)
        rows_here = pl.ds(base, BLOCK)
        factor = inverse_factor(corner, BLOCK)
        update(scaled, base - BLOCK)
        band = work[rows_here, :]
        inside = (lane >= base) & (lane < base + BLOCK)
        band = jnp.where(inside, jnp.where(lane - base == row, -1.0, 0.0), band)
        then = jnp.minimum(base + BLOCK, size - BLOCK)
        tile = pl.multiple_of(then // LANES * LANES, LANES)
        shift = LANES - lax.rem(then, LANES)
        own = band[:, :LANES]
        for t in range(LANES, size, LANES):
            own = jnp.where(then >= t, band[:, t : t + LANES], own)
        own = pltpu.roll(own, shift, axis=1)
        corner = pltpu.roll(work[pl.ds(pl.multiple_of(then, BLOCK), BLOCK), pl.ds(tile, LANES)], shift, axis=1)
        own = by_factor(factor, own)
        corner = corner - by_columns(own, own)[:BLOCK, :]
        scaled = by_factor(factor, band)
        for i, part in enumerate(split(cols_ref[rows_here, :])):
            cols_parts[i, rows_here, :] = part
        for i, part in enumerate(split(gram[rows_here, :])):
            gram_parts[i, rows_here, :] = part
        return scaled, corner

    nothing = jnp.zeros((BLOCK, size), jnp.float32)
    scaled, _ = lax.fori_loop(0, size // BLOCK, sweep, (nothing, core[:BLOCK, :LANES]))
    update(scaled, size - BLOCK)
    for i, part in enumerate(split(-work[...])):
        inverse_parts[i] = part

    def by(ref, x):
        return by_parts(x, (ref[0], ref[1], ref[2]))

    def iterate(step, carry):
        image, pushed = carry
        small = dot(image, pushed, ROWS_BY_ROWS)
        small = jnp.concatenate([small, jnp.zeros((rank, LANES - rank), jnp.float32)], axis=1)
        factor = inverse_factor(small, rank)
        top = jnp.max(jnp.max(jnp.abs(pushed), axis=0, keepdims=True), axis=1, keepdims=True)
        ahead = by(inverse_parts, pushed * (1.0 / top))
        ahead_pushed = by(gram_parts, ahead)
        basis[...] = by_factor(factor, image)
        scaled_factor = factor * top
        return by_factor(scaled_factor, ahead), by_factor(scaled_factor, ahead_pushed)

    image = by(inverse_parts, by(gram_parts, start_ref[...]))
    lax.fori_loop(0, ITERS, iterate, (image, by(gram_parts, image)))
    out_ref[...] = by(cols_parts, basis[...])


def solve(packed, start, cols, voxels):
    size, width = cols.shape
    rank = start.shape[0]
    return pl.pallas_call(
        functools.partial(solve_kernel, voxels),
        out_shape=jax.ShapeDtypeStruct((rank, width), jnp.float32),
        in_specs=[pl.BlockSpec(memory_space=pltpu.VMEM)] * 3,
        out_specs=pl.BlockSpec(memory_space=pltpu.VMEM),
        scratch_shapes=[
            pltpu.VMEM((size, size), jnp.float32),
            pltpu.VMEM((size, size), jnp.float32),
            pltpu.VMEM((rank, size), jnp.float32),
            pltpu.VMEM((3, size, size), jnp.bfloat16),
            pltpu.VMEM((3, size, size), jnp.bfloat16),
            pltpu.VMEM((3, size, width), jnp.bfloat16),
        ],
        compiler_params=pltpu.CompilerParams(vmem_limit_bytes=32 * 2**20),
        name="solve",
    )(packed, start, cols)


def sum_everywhere(pieces):
    far, subs, width = pieces.shape
    near = lax.axis_size(NEAR)
    piece = jnp.sum(lax.all_to_all(pieces, FAR, 0, 0, tiled=True), axis=0)
    copies = jnp.broadcast_to(piece[None], (near, subs, width))
    piece = jnp.sum(lax.all_to_all(copies, NEAR, 0, 0, tiled=True), axis=0)
    copies = jnp.broadcast_to(piece[None], (far, subs, width))
    return lax.all_to_all(copies, FAR, 0, 0, tiled=True)


def body(columns, pivots, start):
    width = columns.shape[1] // lax.axis_size("panel")
    voxels = width * lax.axis_size(ROWS + ("panel",))
    cols = lax.all_to_all(columns, "panel", 1, 0, tiled=True)
    packed = sum_everywhere(pack(cols, pivots, lax.axis_size(FAR)))
    return solve(packed, start.T, cols, voxels)


def solution(mesh):
    fine = Mesh(mesh.devices.reshape(8, 8, 2, 4), ROWS + ("panel",))
    return jax.shard_map(
        body,
        mesh=fine,
        in_specs=(P("panel", ROWS), P(), P()),
        out_specs=P(None, ROWS + ("panel",)),
        check_vma=False,
    )
```

```python
import functools

import jax
import jax.numpy as jnp
from jax import lax
from jax.experimental import pallas as pl
from jax.experimental.pallas import tpu as pltpu
from jax.sharding import Mesh, PartitionSpec as P

ITERS = 3
CORE_SHIFT = 0.1
HIGHEST = lax.Precision.HIGHEST
SUB = 8
LANES = 128
BLOCK = 32
PANEL = 16
EARLY = 4
SUBS = 1

FAR = ("panel", "y")
NEAR = ("z", "core")
ROWS = ("z", "y", "core")


ROWS_BY_COLS = (((1,), (0,)), ((), ()))
ROWS_BY_ROWS = (((1,), (1,)), ((), ()))
COLS_BY_COLS = (((0,), (0,)), ((), ()))

LEFT = (0, 0, 1, 0, 2, 1)
RIGHT = (0, 1, 0, 2, 0, 1)


def dot(a, b, dims=ROWS_BY_COLS):
    return lax.dot_general(a, b, dims, precision=HIGHEST, preferred_element_type=jnp.float32)


def split(x):
    first = x.astype(jnp.bfloat16)
    rest = x - first.astype(jnp.float32)
    second = rest.astype(jnp.bfloat16)
    return first, second, (rest - second.astype(jnp.float32)).astype(jnp.bfloat16)


def stack_rows(x, order):
    parts = split(x)
    return jnp.concatenate([parts[i] for i in order], axis=0)


def by_parts(x, parts):
    n = x.shape[0]
    lhs = jnp.concatenate(split(x), axis=0)
    r0 = jnp.dot(lhs, parts[0], preferred_element_type=jnp.float32)
    r1 = jnp.dot(lhs[: 2 * n], parts[1], preferred_element_type=jnp.float32)
    r2 = jnp.dot(lhs[:n], parts[2], preferred_element_type=jnp.float32)
    return r0[:n] + ((r0[n : 2 * n] + r1[:n]) + (r0[2 * n :] + r1[n:] + r2))


def by_factor(factor, x):
    size = x.shape[0]
    first, second, third = [t.astype(jnp.float32) for t in split(factor)]
    group = lax.broadcasted_iota(jnp.int32, factor.shape, 1) // size
    left = jnp.where(group == 0, 0.0, jnp.where(group == 3, second, first))
    right = jnp.where(group == 0, 0.0, jnp.where(group == 3, second, jnp.where(group == 2, third, first)))
    lhs = jnp.concatenate([left, right], axis=1).astype(jnp.bfloat16)
    return jnp.dot(lhs, stack_rows(x, (0, 0, 1, 0, 0, 2, 0, 1)), preferred_element_type=jnp.float32)


def by_columns(x, y):
    return lax.dot_general(
        stack_rows(x, LEFT), stack_rows(y, RIGHT), COLS_BY_COLS, preferred_element_type=jnp.float32
    )


def inverse_factor(square, size):
    blocks = size // SUB
    row = lax.broadcasted_iota(jnp.int32, (SUB, LANES), 0)
    lane = lax.broadcasted_iota(jnp.int32, (SUB, LANES), 1)

    def spread(tile, r):
        return jnp.broadcast_to(tile[r : r + 1, :], (SUB, LANES))

    rows = []
    for q in range(blocks):
        unit = jnp.where(lane % size == row + SUB * q, 1.0, 0.0)
        rows.append(jnp.where(lane < size, square[SUB * q : SUB * q + SUB, :], unit))
    pivots = [jnp.zeros((SUB, LANES), jnp.float32) for _ in range(blocks)]
    cols = {}

    def take(first):
        for j in range(first, min(first + PANEL, size)):
            for q in range(j // SUB, blocks):
                cols[j, q] = jnp.broadcast_to(rows[q][:, j : j + 1], (SUB, LANES))

    take(0)
    pivot = spread(cols[0, 0], 0)
    taken = PANEL
    for k in range(size):
        if k + EARLY == taken and taken < size:
            take(taken)
            taken += PANEL
        kq, kr = divmod(k, SUB)
        rough = pl.reciprocal(pivot, approx=True)
        near_one = pivot * rough
        recip = rough * (2.0 - near_one)
        pivots[kq] = jnp.where(row == kr, pivot, pivots[kq])
        if k + 1 < size:
            nq, nr = divmod(k + 1, SUB)
            beside = spread(cols[k, nq], nr)
            square_rough = (beside * beside) * rough
            pivot = spread(cols[k + 1, nq], nr) - square_rough * (2.0 - near_one)
        lower = {q: cols[k, q] for q in range(kq, blocks)}
        lower[kq] = jnp.where(row > kr, lower[kq], 0.0)
        lower = {q: t * recip for q, t in lower.items()}
        for j in range(k + 1, min(taken, size)):
            jq, jr = divmod(j, SUB)
            factor = spread(cols[k, jq], jr)
            for q in range(jq, blocks):
                cols[j, q] = cols[j, q] - lower[q] * factor
        above = spread(rows[kq], kr)
        for q in range(kq, blocks):
            rows[q] = rows[q] - lower[q] * above
    return jnp.concatenate([t * lax.rsqrt(p) for t, p in zip(rows, pivots)], axis=0)


def chosen_here(pivots_ref, width):
    place = lax.axis_index(ROWS + ("panel",))
    lane = lax.broadcasted_iota(jnp.int32, (LANES, LANES), 1).astype(jnp.float32)
    chosen = []
    for first in range(0, width, LANES):
        chosen.append(jnp.zeros((LANES, LANES), jnp.float32))
    for group in range(pivots_ref.shape[0]):
        here = (pivots_ref[group : group + 1, :] - place * width).astype(jnp.float32)
        here = jnp.broadcast_to(here, (LANES, LANES)).T
        for i in range(len(chosen)):
            chosen[i] = jnp.where(here == lane + float(i * LANES), 1.0, chosen[i])
    return jnp.concatenate([jnp.max(c, axis=0, keepdims=True) for c in chosen], axis=1)


def pack_kernel(cols_ref, pivots_ref, out_ref):
    far, subs, width = out_ref.shape
    size = cols_ref.shape[0]
    each = size // far // subs
    row = lax.broadcasted_iota(jnp.int32, (size, size), 0)
    lane = lax.broadcasted_iota(jnp.int32, (size, size), 1)
    high, middle, low = split(cols_ref[...])
    chosen = chosen_here(pivots_ref, cols_ref.shape[1]).astype(jnp.bfloat16)
    first = jnp.concatenate([high, high * chosen], axis=0)
    second = jnp.concatenate([middle, middle * chosen], axis=0)

    def product(x, y):
        return lax.dot_general(x, y, ROWS_BY_ROWS, preferred_element_type=jnp.float32)

    mirrored = product(first, low) + product(first, middle)
    plain = product(second, middle) + product(first, high)
    gram_half, core_half = mirrored[:size], mirrored[size:]
    turned = jnp.where(row <= lane, gram_half, core_half).T
    packed = jnp.where(row >= lane, plain[:size] + gram_half, plain[size:] + core_half) + turned
    core_diagonal = plain[size:] + 2.0 * core_half
    diagonal = jnp.sum(jnp.where(row == lane, core_diagonal, 0.0), axis=1, keepdims=True)
    spare = width - each * size
    spare_lane = lax.broadcasted_iota(jnp.int32, (far, spare), 1)
    for r in range(subs):
        tail = jnp.zeros((far, spare), jnp.float32)
        for h in range(each):
            at = (r * each + h) * far
            out_ref[:, r, h * size : (h + 1) * size] = packed[at : at + far, :]
            tail = jnp.where(spare_lane == h, diagonal[at : at + far, :], tail)
        out_ref[:, r, each * size :] = tail


def pack(cols, pivots, far):
    size = cols.shape[0]
    each = size // far // SUBS
    return pl.pallas_call(
        pack_kernel,
        out_shape=jax.ShapeDtypeStruct((far, SUBS, each * size + LANES), jnp.float32),
        in_specs=[pl.BlockSpec(memory_space=pltpu.VMEM)] * 2,
        out_specs=pl.BlockSpec(memory_space=pltpu.VMEM),
        compiler_params=pltpu.CompilerParams(vmem_limit_bytes=32 * 2**20),
        name="pack",
    )(cols, pivots.reshape(-1, LANES))


def solve_kernel(voxels, packed_ref, start_ref, cols_ref, out_ref, work, gram, basis, gram_parts, inverse_parts, cols_parts):
    size = cols_ref.shape[0]
    rank = start_ref.shape[0]
    far, subs, width = packed_ref.shape
    each = size // far // subs
    every_row = lax.broadcasted_iota(jnp.int32, (size, size), 0)
    every_lane = lax.broadcasted_iota(jnp.int32, (size, size), 1)
    rows, diagonal = [], []
    for r in range(subs):
        tail = packed_ref[:, r, each * size :]
        for h in range(each):
            rows.append(packed_ref[:, r, h * size : (h + 1) * size])
            diagonal.append(tail[:, h : h + 1])
    packed = jnp.concatenate(rows, axis=0)
    flipped = packed.T
    gram[...] = jnp.where(every_row >= every_lane, packed, flipped) * (1.0 / voxels)
    core = jnp.where(every_row < every_lane, packed, flipped)
    core = jnp.where(every_row == every_lane, jnp.concatenate(diagonal, axis=0), core) * (1.0 / size)
    core = core + jnp.where(every_row == every_lane, CORE_SHIFT, 0.0)
    work[...] = core

    lane = lax.broadcasted_iota(jnp.int32, (BLOCK, size), 1)
    row = lax.broadcasted_iota(jnp.int32, (BLOCK, size), 0)

    def update(scaled, base):
        keep_row = (every_row < base) | (every_row >= base + BLOCK)
        keep_lane = (every_lane < base) | (every_lane >= base + BLOCK)
        work[...] = jnp.where(keep_row & keep_lane, work[...], 0.0) - by_columns(scaled, scaled)

    def sweep(step, carry):
        scaled, corner = carry
        base = pl.multiple_of(step * BLOCK, BLOCK)
        rows_here = pl.ds(base, BLOCK)
        factor = inverse_factor(corner, BLOCK)
        update(scaled, base - BLOCK)
        band = work[rows_here, :]
        inside = (lane >= base) & (lane < base + BLOCK)
        band = jnp.where(inside, jnp.where(lane - base == row, -1.0, 0.0), band)
        then = jnp.minimum(base + BLOCK, size - BLOCK)
        tile = pl.multiple_of(then // LANES * LANES, LANES)
        shift = LANES - lax.rem(then, LANES)
        own = band[:, :LANES]
        for t in range(LANES, size, LANES):
            own = jnp.where(then >= t, band[:, t : t + LANES], own)
        own = pltpu.roll(own, shift, axis=1)
        corner = pltpu.roll(work[pl.ds(pl.multiple_of(then, BLOCK), BLOCK), pl.ds(tile, LANES)], shift, axis=1)
        own = by_factor(factor, own)
        corner = corner - by_columns(own, own)[:BLOCK, :]
        scaled = by_factor(factor, band)
        for i, part in enumerate(split(cols_ref[rows_here, :])):
            cols_parts[i, rows_here, :] = part
        for i, part in enumerate(split(gram[rows_here, :])):
            gram_parts[i, rows_here, :] = part
        return scaled, corner

    nothing = jnp.zeros((BLOCK, size), jnp.float32)
    scaled, _ = lax.fori_loop(0, size // BLOCK, sweep, (nothing, core[:BLOCK, :LANES]))
    update(scaled, size - BLOCK)
    for i, part in enumerate(split(-work[...])):
        inverse_parts[i] = part

    def by(ref, x):
        return by_parts(x, (ref[0], ref[1], ref[2]))

    def iterate(step, carry):
        image, pushed = carry
        small = dot(image, pushed, ROWS_BY_ROWS)
        small = jnp.concatenate([small, jnp.zeros((rank, LANES - rank), jnp.float32)], axis=1)
        factor = inverse_factor(small, rank)
        top = jnp.max(jnp.max(jnp.abs(pushed), axis=0, keepdims=True), axis=1, keepdims=True)
        ahead = by(inverse_parts, pushed * (1.0 / top))
        ahead_pushed = by(gram_parts, ahead)
        basis[...] = by_factor(factor, image)
        scaled_factor = factor * top
        return by_factor(scaled_factor, ahead), by_factor(scaled_factor, ahead_pushed)

    image = by(inverse_parts, by(gram_parts, start_ref[...]))
    lax.fori_loop(0, ITERS, iterate, (image, by(gram_parts, image)))
    out_ref[...] = by(cols_parts, basis[...])


def solve(packed, start, cols, voxels):
    size, width = cols.shape
    rank = start.shape[0]
    return pl.pallas_call(
        functools.partial(solve_kernel, voxels),
        out_shape=jax.ShapeDtypeStruct((rank, width), jnp.float32),
        in_specs=[pl.BlockSpec(memory_space=pltpu.VMEM)] * 3,
        out_specs=pl.BlockSpec(memory_space=pltpu.VMEM),
        scratch_shapes=[
            pltpu.VMEM((size, size), jnp.float32),
            pltpu.VMEM((size, size), jnp.float32),
            pltpu.VMEM((rank, size), jnp.float32),
            pltpu.VMEM((3, size, size), jnp.bfloat16),
            pltpu.VMEM((3, size, size), jnp.bfloat16),
            pltpu.VMEM((3, size, width), jnp.bfloat16),
        ],
        compiler_params=pltpu.CompilerParams(vmem_limit_bytes=32 * 2**20),
        name="solve",
    )(packed, start, cols)


def sum_everywhere(pieces):
    far, subs, width = pieces.shape
    near = lax.axis_size(NEAR)
    piece = jnp.sum(lax.all_to_all(pieces, FAR, 0, 0, tiled=True), axis=0)
    copies = jnp.broadcast_to(piece[None], (near, subs, width))
    piece = jnp.sum(lax.all_to_all(copies, NEAR, 0, 0, tiled=True), axis=0)
    copies = jnp.broadcast_to(piece[None], (far, subs, width))
    return lax.all_to_all(copies, FAR, 0, 0, tiled=True)


def body(columns, pivots, start):
    width = columns.shape[1] // lax.axis_size("panel")
    voxels = width * lax.axis_size(ROWS + ("panel",))
    cols = lax.all_to_all(columns, "panel", 1, 0, tiled=True)
    packed = sum_everywhere(pack(cols, pivots, lax.axis_size(FAR)))
    return solve(packed, start.T, cols, voxels)


def solution(mesh):
    fine = Mesh(mesh.devices.reshape(8, 8, 2, 4), ROWS + ("panel",))
    return jax.shard_map(
        body,
        mesh=fine,
        in_specs=(P("panel", ROWS), P(), P()),
        out_specs=P(None, ROWS + ("panel",)),
        check_vma=False,
    )
```

```python
import functools

import jax
import jax.numpy as jnp
from jax import lax
from jax.experimental import pallas as pl
from jax.experimental.pallas import tpu as pltpu
from jax.sharding import Mesh, PartitionSpec as P

ITERS = 3
CORE_SHIFT = 0.1
HIGHEST = lax.Precision.HIGHEST
SUB = 8
LANES = 128
BLOCK = 32
PANEL = 16
EARLY = 4
SUBS = 1

FAR = ("panel", "z")
NEAR = ("y", "core")
ROWS = ("z", "y", "core")


ROWS_BY_COLS = (((1,), (0,)), ((), ()))
ROWS_BY_ROWS = (((1,), (1,)), ((), ()))
COLS_BY_COLS = (((0,), (0,)), ((), ()))

LEFT = (0, 0, 1, 0, 2, 1)
RIGHT = (0, 1, 0, 2, 0, 1)


def dot(a, b, dims=ROWS_BY_COLS):
    return lax.dot_general(a, b, dims, precision=HIGHEST, preferred_element_type=jnp.float32)


def split(x):
    first = x.astype(jnp.bfloat16)
    rest = x - first.astype(jnp.float32)
    second = rest.astype(jnp.bfloat16)
    return first, second, (rest - second.astype(jnp.float32)).astype(jnp.bfloat16)


def stack_rows(x, order):
    parts = split(x)
    return jnp.concatenate([parts[i] for i in order], axis=0)


def by_parts(x, parts):
    n = x.shape[0]
    lhs = jnp.concatenate(split(x), axis=0)
    r0 = jnp.dot(lhs, parts[0], preferred_element_type=jnp.float32)
    r1 = jnp.dot(lhs[: 2 * n], parts[1], preferred_element_type=jnp.float32)
    r2 = jnp.dot(lhs[:n], parts[2], preferred_element_type=jnp.float32)
    return r0[:n] + ((r0[n : 2 * n] + r1[:n]) + (r0[2 * n :] + r1[n:] + r2))


def by_factor(factor, x):
    size = x.shape[0]
    first, second, third = [t.astype(jnp.float32) for t in split(factor)]
    group = lax.broadcasted_iota(jnp.int32, factor.shape, 1) // size
    left = jnp.where(group == 0, 0.0, jnp.where(group == 3, second, first))
    right = jnp.where(group == 0, 0.0, jnp.where(group == 3, second, jnp.where(group == 2, third, first)))
    lhs = jnp.concatenate([left, right], axis=1).astype(jnp.bfloat16)
    return jnp.dot(lhs, stack_rows(x, (0, 0, 1, 0, 0, 2, 0, 1)), preferred_element_type=jnp.float32)


def by_columns(x, y):
    return lax.dot_general(
        stack_rows(x, LEFT), stack_rows(y, RIGHT), COLS_BY_COLS, preferred_element_type=jnp.float32
    )


def inverse_factor(square, size):
    blocks = size // SUB
    row = lax.broadcasted_iota(jnp.int32, (SUB, LANES), 0)
    lane = lax.broadcasted_iota(jnp.int32, (SUB, LANES), 1)

    def spread(tile, r):
        return jnp.broadcast_to(tile[r : r + 1, :], (SUB, LANES))

    rows = []
    for q in range(blocks):
        unit = jnp.where(lane % size == row + SUB * q, 1.0, 0.0)
        rows.append(jnp.where(lane < size, square[SUB * q : SUB * q + SUB, :], unit))
    pivots = [jnp.zeros((SUB, LANES), jnp.float32) for _ in range(blocks)]
    cols = {}

    def take(first):
        for j in range(first, min(first + PANEL, size)):
            for q in range(j // SUB, blocks):
                cols[j, q] = jnp.broadcast_to(rows[q][:, j : j + 1], (SUB, LANES))

    take(0)
    pivot = spread(cols[0, 0], 0)
    taken = PANEL
    for k in range(size):
        if k + EARLY == taken and taken < size:
            take(taken)
            taken += PANEL
        kq, kr = divmod(k, SUB)
        rough = pl.reciprocal(pivot, approx=True)
        near_one = pivot * rough
        recip = rough * (2.0 - near_one)
        pivots[kq] = jnp.where(row == kr, pivot, pivots[kq])
        if k + 1 < size:
            nq, nr = divmod(k + 1, SUB)
            beside = spread(cols[k, nq], nr)
            square_rough = beside * (beside * rough)
            pivot = spread(cols[k + 1, nq], nr) - square_rough * (2.0 - near_one)
        lower = {q: cols[k, q] for q in range(kq, blocks)}
        lower[kq] = jnp.where(row > kr, lower[kq], 0.0)
        lower = {q: t * recip for q, t in lower.items()}
        for j in range(k + 1, min(taken, size)):
            jq, jr = divmod(j, SUB)
            factor = spread(cols[k, jq], jr)
            for q in range(jq, blocks):
                cols[j, q] = cols[j, q] - lower[q] * factor
        above = spread(rows[kq], kr)
        for q in range(kq, blocks):
            rows[q] = rows[q] - lower[q] * above
    return jnp.concatenate([t * lax.rsqrt(p) for t, p in zip(rows, pivots)], axis=0)


def chosen_here(pivots_ref, width):
    place = lax.axis_index(ROWS + ("panel",))
    lane = lax.broadcasted_iota(jnp.int32, (LANES, LANES), 1).astype(jnp.float32)
    chosen = []
    for first in range(0, width, LANES):
        chosen.append(jnp.zeros((LANES, LANES), jnp.float32))
    for group in range(pivots_ref.shape[0]):
        here = (pivots_ref[group : group + 1, :] - place * width).astype(jnp.float32)
        here = jnp.broadcast_to(here, (LANES, LANES)).T
        for i in range(len(chosen)):
            chosen[i] = jnp.where(here == lane + float(i * LANES), 1.0, chosen[i])
    return jnp.concatenate([jnp.max(c, axis=0, keepdims=True) for c in chosen], axis=1)


def pack_kernel(cols_ref, pivots_ref, out_ref):
    far, subs, width = out_ref.shape
    size = cols_ref.shape[0]
    each = size // far // subs
    row = lax.broadcasted_iota(jnp.int32, (size, size), 0)
    lane = lax.broadcasted_iota(jnp.int32, (size, size), 1)
    high, middle, low = split(cols_ref[...])
    chosen = chosen_here(pivots_ref, cols_ref.shape[1]).astype(jnp.bfloat16)
    first = jnp.concatenate([high, high * chosen], axis=0)
    second = jnp.concatenate([middle, middle * chosen], axis=0)

    def product(x, y):
        return lax.dot_general(x, y, ROWS_BY_ROWS, preferred_element_type=jnp.float32)

    mirrored = product(first, low) + product(first, middle)
    plain = product(second, middle) + product(first, high)
    gram_half, core_half = mirrored[:size], mirrored[size:]
    turned = jnp.where(row <= lane, gram_half, core_half).T
    packed = jnp.where(row >= lane, plain[:size] + gram_half, plain[size:] + core_half) + turned
    core_diagonal = plain[size:] + 2.0 * core_half
    diagonal = jnp.sum(jnp.where(row == lane, core_diagonal, 0.0), axis=1, keepdims=True)
    spare = width - each * size
    spare_lane = lax.broadcasted_iota(jnp.int32, (far, spare), 1)
    for r in range(subs):
        tail = jnp.zeros((far, spare), jnp.float32)
        for h in range(each):
            at = (r * each + h) * far
            out_ref[:, r, h * size : (h + 1) * size] = packed[at : at + far, :]
            tail = jnp.where(spare_lane == h, diagonal[at : at + far, :], tail)
        out_ref[:, r, each * size :] = tail


def pack(cols, pivots, far):
    size = cols.shape[0]
    each = size // far // SUBS
    return pl.pallas_call(
        pack_kernel,
        out_shape=jax.ShapeDtypeStruct((far, SUBS, each * size + LANES), jnp.float32),
        in_specs=[pl.BlockSpec(memory_space=pltpu.VMEM)] * 2,
        out_specs=pl.BlockSpec(memory_space=pltpu.VMEM),
        compiler_params=pltpu.CompilerParams(vmem_limit_bytes=32 * 2**20),
        name="pack",
    )(cols, pivots.reshape(-1, LANES))


def solve_kernel(voxels, packed_ref, start_ref, cols_ref, out_ref, work, gram, gram_parts, inverse_parts, cols_parts):
    size = cols_ref.shape[0]
    rank = start_ref.shape[0]
    far, subs, width = packed_ref.shape
    each = size // far // subs
    every_row = lax.broadcasted_iota(jnp.int32, (size, size), 0)
    every_lane = lax.broadcasted_iota(jnp.int32, (size, size), 1)
    rows, diagonal = [], []
    for r in range(subs):
        tail = packed_ref[:, r, each * size :]
        for h in range(each):
            rows.append(packed_ref[:, r, h * size : (h + 1) * size])
            diagonal.append(tail[:, h : h + 1])
    packed = jnp.concatenate(rows, axis=0)
    flipped = packed.T
    gram[...] = jnp.where(every_row >= every_lane, packed, flipped) * (1.0 / voxels)
    core = jnp.where(every_row < every_lane, packed, flipped)
    core = jnp.where(every_row == every_lane, jnp.concatenate(diagonal, axis=0), core) * (1.0 / size)
    core = core + jnp.where(every_row == every_lane, CORE_SHIFT, 0.0)
    work[...] = core

    lane = lax.broadcasted_iota(jnp.int32, (BLOCK, size), 1)
    row = lax.broadcasted_iota(jnp.int32, (BLOCK, size), 0)

    def update(scaled, base):
        keep_row = (every_row < base) | (every_row >= base + BLOCK)
        keep_lane = (every_lane < base) | (every_lane >= base + BLOCK)
        work[...] = jnp.where(keep_row & keep_lane, work[...], 0.0) - by_columns(scaled, scaled)

    def sweep(step, carry):
        scaled, corner = carry
        base = pl.multiple_of(step * BLOCK, BLOCK)
        rows_here = pl.ds(base, BLOCK)
        factor = inverse_factor(corner, BLOCK)
        update(scaled, base - BLOCK)
        band = work[rows_here, :]
        inside = (lane >= base) & (lane < base + BLOCK)
        band = jnp.where(inside, jnp.where(lane - base == row, -1.0, 0.0), band)
        then = jnp.minimum(base + BLOCK, size - BLOCK)
        tile = pl.multiple_of(then // LANES * LANES, LANES)
        shift = LANES - lax.rem(then, LANES)
        own = band[:, :LANES]
        for t in range(LANES, size, LANES):
            own = jnp.where(then >= t, band[:, t : t + LANES], own)
        own = pltpu.roll(own, shift, axis=1)
        corner = pltpu.roll(work[pl.ds(pl.multiple_of(then, BLOCK), BLOCK), pl.ds(tile, LANES)], shift, axis=1)
        own = by_factor(factor, own)
        corner = corner - by_columns(own, own)[:BLOCK, :]
        scaled = by_factor(factor, band)
        for i, part in enumerate(split(cols_ref[rows_here, :])):
            cols_parts[i, rows_here, :] = part
        for i, part in enumerate(split(gram[rows_here, :])):
            gram_parts[i, rows_here, :] = part
        return scaled, corner

    nothing = jnp.zeros((BLOCK, size), jnp.float32)
    scaled, _ = lax.fori_loop(0, size // BLOCK, sweep, (nothing, core[:BLOCK, :LANES]))
    update(scaled, size - BLOCK)
    for i, part in enumerate(split(-work[...])):
        inverse_parts[i] = part

    def by(ref, x):
        return by_parts(x, (ref[0], ref[1], ref[2]))

    def factor_of(image, pushed):
        small = dot(image, pushed, ROWS_BY_ROWS)
        small = jnp.concatenate([small, jnp.zeros((rank, LANES - rank), jnp.float32)], axis=1)
        return inverse_factor(small, rank)

    def iterate(step, carry):
        image, pushed = carry
        factor = factor_of(image, pushed)
        top = jnp.max(jnp.max(jnp.abs(pushed), axis=0, keepdims=True), axis=1, keepdims=True)
        ahead = by(inverse_parts, pushed * (1.0 / top))
        ahead_pushed = by(gram_parts, ahead)
        scaled_factor = factor * top
        return by_factor(scaled_factor, ahead), by_factor(scaled_factor, ahead_pushed)

    image = by(inverse_parts, by(gram_parts, start_ref[...]))
    image, pushed = lax.fori_loop(0, ITERS - 1, iterate, (image, by(gram_parts, image)))
    volumes = by(cols_parts, image)
    out_ref[...] = by_factor(factor_of(image, pushed), volumes)


def solve(packed, start, cols, voxels):
    size, width = cols.shape
    rank = start.shape[0]
    return pl.pallas_call(
        functools.partial(solve_kernel, voxels),
        out_shape=jax.ShapeDtypeStruct((rank, width), jnp.float32),
        in_specs=[pl.BlockSpec(memory_space=pltpu.VMEM)] * 3,
        out_specs=pl.BlockSpec(memory_space=pltpu.VMEM),
        scratch_shapes=[
            pltpu.VMEM((size, size), jnp.float32),
            pltpu.VMEM((size, size), jnp.float32),
            pltpu.VMEM((3, size, size), jnp.bfloat16),
            pltpu.VMEM((3, size, size), jnp.bfloat16),
            pltpu.VMEM((3, size, width), jnp.bfloat16),
        ],
        compiler_params=pltpu.CompilerParams(vmem_limit_bytes=32 * 2**20),
        name="solve",
    )(packed, start, cols)


def sum_everywhere(pieces):
    far, subs, width = pieces.shape
    near = lax.axis_size(NEAR)
    piece = jnp.sum(lax.all_to_all(pieces, FAR, 0, 0, tiled=True), axis=0)
    copies = jnp.broadcast_to(piece[None], (near, subs, width))
    piece = jnp.sum(lax.all_to_all(copies, NEAR, 0, 0, tiled=True), axis=0)
    copies = jnp.broadcast_to(piece[None], (far, subs, width))
    return lax.all_to_all(copies, FAR, 0, 0, tiled=True)


def body(columns, pivots, start):
    width = columns.shape[1] // lax.axis_size("panel")
    voxels = width * lax.axis_size(ROWS + ("panel",))
    cols = lax.all_to_all(columns, "panel", 1, 0, tiled=True)
    packed = sum_everywhere(pack(cols, pivots, lax.axis_size(FAR)))
    return solve(packed, start.T, cols, voxels)


def solution(mesh):
    fine = Mesh(mesh.devices.reshape(8, 8, 2, 4), ROWS + ("panel",))
    return jax.shard_map(
        body,
        mesh=fine,
        in_specs=(P("panel", ROWS), P(), P()),
        out_specs=P(None, ROWS + ("panel",)),
        check_vma=False,
    )
```

```python
import functools

import jax
import jax.numpy as jnp
from jax import lax
from jax.experimental import pallas as pl
from jax.experimental.pallas import tpu as pltpu
from jax.sharding import Mesh, PartitionSpec as P

ITERS = 3
CORE_SHIFT = 0.1
HIGHEST = lax.Precision.HIGHEST
SUB = 8
LANES = 128
BLOCK = 32
PANEL = 16
EARLY = 4
SUBS = 1

FAR = ("panel", "z")
NEAR = ("core", "y")
ROWS = ("z", "y", "core")


ROWS_BY_COLS = (((1,), (0,)), ((), ()))
ROWS_BY_ROWS = (((1,), (1,)), ((), ()))
COLS_BY_COLS = (((0,), (0,)), ((), ()))

LEFT = (0, 0, 1, 0, 2, 1)
RIGHT = (0, 1, 0, 2, 0, 1)


def dot(a, b, dims=ROWS_BY_COLS):
    return lax.dot_general(a, b, dims, precision=HIGHEST, preferred_element_type=jnp.float32)


def split(x):
    first = x.astype(jnp.bfloat16)
    rest = x - first.astype(jnp.float32)
    second = rest.astype(jnp.bfloat16)
    return first, second, (rest - second.astype(jnp.float32)).astype(jnp.bfloat16)


def stack_rows(x, order):
    parts = split(x)
    return jnp.concatenate([parts[i] for i in order], axis=0)


def by_parts(x, parts):
    n = x.shape[0]
    lhs = jnp.concatenate(split(x), axis=0)
    r0 = jnp.dot(lhs, parts[0], preferred_element_type=jnp.float32)
    r1 = jnp.dot(lhs[: 2 * n], parts[1], preferred_element_type=jnp.float32)
    r2 = jnp.dot(lhs[:n], parts[2], preferred_element_type=jnp.float32)
    return r0[:n] + ((r0[n : 2 * n] + r1[:n]) + (r0[2 * n :] + r1[n:] + r2))


def by_factor(factor, x):
    size = x.shape[0]
    first, second, third = [t.astype(jnp.float32) for t in split(factor)]
    group = lax.broadcasted_iota(jnp.int32, factor.shape, 1) // size
    left = jnp.where(group == 0, 0.0, jnp.where(group == 3, second, first))
    right = jnp.where(group == 0, 0.0, jnp.where(group == 3, second, jnp.where(group == 2, third, first)))
    lhs = jnp.concatenate([left, right], axis=1).astype(jnp.bfloat16)
    return jnp.dot(lhs, stack_rows(x, (0, 0, 1, 0, 0, 2, 0, 1)), preferred_element_type=jnp.float32)


def by_columns(x, y):
    return lax.dot_general(
        stack_rows(x, LEFT), stack_rows(y, RIGHT), COLS_BY_COLS, preferred_element_type=jnp.float32
    )


def inverse_factor(square, size):
    blocks = size // SUB
    row = lax.broadcasted_iota(jnp.int32, (SUB, LANES), 0)
    lane = lax.broadcasted_iota(jnp.int32, (SUB, LANES), 1)

    def spread(tile, r):
        return jnp.broadcast_to(tile[r : r + 1, :], (SUB, LANES))

    rows = []
    for q in range(blocks):
        unit = jnp.where(lane % size == row + SUB * q, 1.0, 0.0)
        rows.append(jnp.where(lane < size, square[SUB * q : SUB * q + SUB, :], unit))
    pivots = [jnp.zeros((SUB, LANES), jnp.float32) for _ in range(blocks)]
    cols = {}

    def take(first):
        for j in range(first, min(first + PANEL, size)):
            for q in range(j // SUB, blocks):
                cols[j, q] = jnp.broadcast_to(rows[q][:, j : j + 1], (SUB, LANES))

    take(0)
    pivot = spread(cols[0, 0], 0)
    taken = PANEL
    for k in range(size):
        if k + EARLY == taken and taken < size:
            take(taken)
            taken += PANEL
        kq, kr = divmod(k, SUB)
        rough = pl.reciprocal(pivot, approx=True)
        near_one = pivot * rough
        recip = rough * (2.0 - near_one)
        pivots[kq] = jnp.where(row == kr, pivot, pivots[kq])
        if k + 1 < size:
            nq, nr = divmod(k + 1, SUB)
            beside = spread(cols[k, nq], nr)
            square_rough = beside * (beside * rough)
            pivot = spread(cols[k + 1, nq], nr) - square_rough * (2.0 - near_one)
        lower = {q: cols[k, q] for q in range(kq, blocks)}
        lower[kq] = jnp.where(row > kr, lower[kq], 0.0)
        lower = {q: t * recip for q, t in lower.items()}
        for j in range(k + 1, min(taken, size)):
            jq, jr = divmod(j, SUB)
            factor = spread(cols[k, jq], jr)
            for q in range(jq, blocks):
                cols[j, q] = cols[j, q] - lower[q] * factor
        above = spread(rows[kq], kr)
        for q in range(kq, blocks):
            rows[q] = rows[q] - lower[q] * above
    return jnp.concatenate([t * lax.rsqrt(p) for t, p in zip(rows, pivots)], axis=0)


def chosen_here(pivots_ref, width):
    place = lax.axis_index(ROWS + ("panel",))
    lane = lax.broadcasted_iota(jnp.int32, (LANES, LANES), 1).astype(jnp.float32)
    chosen = []
    for first in range(0, width, LANES):
        chosen.append(jnp.zeros((LANES, LANES), jnp.float32))
    for group in range(pivots_ref.shape[0]):
        here = (pivots_ref[group : group + 1, :] - place * width).astype(jnp.float32)
        here = jnp.broadcast_to(here, (LANES, LANES)).T
        for i in range(len(chosen)):
            chosen[i] = jnp.where(here == lane + float(i * LANES), 1.0, chosen[i])
    return jnp.concatenate([jnp.max(c, axis=0, keepdims=True) for c in chosen], axis=1)


def pack_kernel(cols_ref, pivots_ref, out_ref):
    far, subs, width = out_ref.shape
    size = cols_ref.shape[0]
    each = size // far // subs
    row = lax.broadcasted_iota(jnp.int32, (size, size), 0)
    lane = lax.broadcasted_iota(jnp.int32, (size, size), 1)
    high, middle, low = split(cols_ref[...])
    chosen = chosen_here(pivots_ref, cols_ref.shape[1]).astype(jnp.bfloat16)
    first = jnp.concatenate([high, high * chosen], axis=0)
    second = jnp.concatenate([middle, middle * chosen], axis=0)

    def product(x, y):
        return lax.dot_general(x, y, ROWS_BY_ROWS, preferred_element_type=jnp.float32)

    mirrored = product(first, low) + product(first, middle)
    plain = product(second, middle) + product(first, high)
    gram_half, core_half = mirrored[:size], mirrored[size:]
    turned = jnp.where(row <= lane, gram_half, core_half).T
    packed = jnp.where(row >= lane, plain[:size] + gram_half, plain[size:] + core_half) + turned
    core_diagonal = plain[size:] + 2.0 * core_half
    diagonal = jnp.sum(jnp.where(row == lane, core_diagonal, 0.0), axis=1, keepdims=True)
    spare = width - each * size
    spare_lane = lax.broadcasted_iota(jnp.int32, (far, spare), 1)
    for r in range(subs):
        tail = jnp.zeros((far, spare), jnp.float32)
        for h in range(each):
            at = (r * each + h) * far
            out_ref[:, r, h * size : (h + 1) * size] = packed[at : at + far, :]
            tail = jnp.where(spare_lane == h, diagonal[at : at + far, :], tail)
        out_ref[:, r, each * size :] = tail


def pack(cols, pivots, far):
    size = cols.shape[0]
    each = size // far // SUBS
    return pl.pallas_call(
        pack_kernel,
        out_shape=jax.ShapeDtypeStruct((far, SUBS, each * size + LANES), jnp.float32),
        in_specs=[pl.BlockSpec(memory_space=pltpu.VMEM)] * 2,
        out_specs=pl.BlockSpec(memory_space=pltpu.VMEM),
        compiler_params=pltpu.CompilerParams(vmem_limit_bytes=32 * 2**20),
        name="pack",
    )(cols, pivots.reshape(-1, LANES))


def solve_kernel(voxels, packed_ref, start_ref, cols_ref, out_ref, work, gram, gram_parts, inverse_parts, cols_parts):
    size = cols_ref.shape[0]
    rank = start_ref.shape[0]
    far, subs, width = packed_ref.shape
    each = size // far // subs
    every_row = lax.broadcasted_iota(jnp.int32, (size, size), 0)
    every_lane = lax.broadcasted_iota(jnp.int32, (size, size), 1)
    rows, diagonal = [], []
    for r in range(subs):
        tail = packed_ref[:, r, each * size :]
        for h in range(each):
            rows.append(packed_ref[:, r, h * size : (h + 1) * size])
            diagonal.append(tail[:, h : h + 1])
    packed = jnp.concatenate(rows, axis=0)
    flipped = packed.T
    gram[...] = jnp.where(every_row >= every_lane, packed, flipped) * (1.0 / voxels)
    core = jnp.where(every_row < every_lane, packed, flipped)
    core = jnp.where(every_row == every_lane, jnp.concatenate(diagonal, axis=0), core) * (1.0 / size)
    core = core + jnp.where(every_row == every_lane, CORE_SHIFT, 0.0)
    work[...] = core

    lane = lax.broadcasted_iota(jnp.int32, (BLOCK, size), 1)
    row = lax.broadcasted_iota(jnp.int32, (BLOCK, size), 0)

    def update(scaled, base):
        keep_row = (every_row < base) | (every_row >= base + BLOCK)
        keep_lane = (every_lane < base) | (every_lane >= base + BLOCK)
        work[...] = jnp.where(keep_row & keep_lane, work[...], 0.0) - by_columns(scaled, scaled)

    def sweep(step, carry):
        scaled, corner = carry
        base = pl.multiple_of(step * BLOCK, BLOCK)
        rows_here = pl.ds(base, BLOCK)
        factor = inverse_factor(corner, BLOCK)
        update(scaled, base - BLOCK)
        band = work[rows_here, :]
        inside = (lane >= base) & (lane < base + BLOCK)
        band = jnp.where(inside, jnp.where(lane - base == row, -1.0, 0.0), band)
        then = jnp.minimum(base + BLOCK, size - BLOCK)
        tile = pl.multiple_of(then // LANES * LANES, LANES)
        shift = LANES - lax.rem(then, LANES)
        own = band[:, :LANES]
        for t in range(LANES, size, LANES):
            own = jnp.where(then >= t, band[:, t : t + LANES], own)
        own = pltpu.roll(own, shift, axis=1)
        corner = pltpu.roll(work[pl.ds(pl.multiple_of(then, BLOCK), BLOCK), pl.ds(tile, LANES)], shift, axis=1)
        own = by_factor(factor, own)
        corner = corner - by_columns(own, own)[:BLOCK, :]
        scaled = by_factor(factor, band)
        for i, part in enumerate(split(cols_ref[rows_here, :])):
            cols_parts[i, rows_here, :] = part
        for i, part in enumerate(split(gram[rows_here, :])):
            gram_parts[i, rows_here, :] = part
        return scaled, corner

    nothing = jnp.zeros((BLOCK, size), jnp.float32)
    scaled, _ = lax.fori_loop(0, size // BLOCK, sweep, (nothing, core[:BLOCK, :LANES]))
    update(scaled, size - BLOCK)
    for i, part in enumerate(split(-work[...])):
        inverse_parts[i] = part

    def by(ref, x):
        return by_parts(x, (ref[0], ref[1], ref[2]))

    def factor_of(image, pushed):
        small = dot(image, pushed, ROWS_BY_ROWS)
        small = jnp.concatenate([small, jnp.zeros((rank, LANES - rank), jnp.float32)], axis=1)
        return inverse_factor(small, rank)

    def iterate(step, carry):
        image, pushed = carry
        factor = factor_of(image, pushed)
        top = jnp.max(jnp.max(jnp.abs(pushed), axis=0, keepdims=True), axis=1, keepdims=True)
        ahead = by(inverse_parts, pushed * (1.0 / top))
        ahead_pushed = by(gram_parts, ahead)
        scaled_factor = factor * top
        return by_factor(scaled_factor, ahead), by_factor(scaled_factor, ahead_pushed)

    image = by(inverse_parts, by(gram_parts, start_ref[...]))
    image, pushed = lax.fori_loop(0, ITERS - 1, iterate, (image, by(gram_parts, image)))
    volumes = by(cols_parts, image)
    out_ref[...] = by_factor(factor_of(image, pushed), volumes)


def solve(packed, start, cols, voxels):
    size, width = cols.shape
    rank = start.shape[0]
    return pl.pallas_call(
        functools.partial(solve_kernel, voxels),
        out_shape=jax.ShapeDtypeStruct((rank, width), jnp.float32),
        in_specs=[pl.BlockSpec(memory_space=pltpu.VMEM)] * 3,
        out_specs=pl.BlockSpec(memory_space=pltpu.VMEM),
        scratch_shapes=[
            pltpu.VMEM((size, size), jnp.float32),
            pltpu.VMEM((size, size), jnp.float32),
            pltpu.VMEM((3, size, size), jnp.bfloat16),
            pltpu.VMEM((3, size, size), jnp.bfloat16),
            pltpu.VMEM((3, size, width), jnp.bfloat16),
        ],
        compiler_params=pltpu.CompilerParams(vmem_limit_bytes=32 * 2**20),
        name="solve",
    )(packed, start, cols)


def sum_everywhere(pieces):
    far, subs, width = pieces.shape
    near = lax.axis_size(NEAR)
    piece = jnp.sum(lax.all_to_all(pieces, FAR, 0, 0, tiled=True), axis=0)
    copies = jnp.broadcast_to(piece[None], (near, subs, width))
    piece = jnp.sum(lax.all_to_all(copies, NEAR, 0, 0, tiled=True), axis=0)
    copies = jnp.broadcast_to(piece[None], (far, subs, width))
    return lax.all_to_all(copies, FAR, 0, 0, tiled=True)


def body(columns, pivots, start):
    width = columns.shape[1] // lax.axis_size("panel")
    voxels = width * lax.axis_size(ROWS + ("panel",))
    cols = lax.all_to_all(columns, "panel", 1, 0, tiled=True)
    packed = sum_everywhere(pack(cols, pivots, lax.axis_size(FAR)))
    return solve(packed, start.T, cols, voxels)


def solution(mesh):
    fine = Mesh(mesh.devices.reshape(8, 8, 2, 4), ROWS + ("panel",))
    return jax.shard_map(
        body,
        mesh=fine,
        in_specs=(P("panel", ROWS), P(), P()),
        out_specs=P(None, ROWS + ("panel",)),
        check_vma=False,
    )
```

```python
import functools

import jax
import jax.numpy as jnp
from jax import lax
from jax.experimental import pallas as pl
from jax.experimental.pallas import tpu as pltpu
from jax.sharding import Mesh, PartitionSpec as P

ITERS = 3
CORE_SHIFT = 0.1
HIGHEST = lax.Precision.HIGHEST
SUB = 8
LANES = 128
BLOCK = 32
PANEL = 16
EARLY = 4
SUBS = 1

FAR = ("panel", "z")
NEAR = ("core", "y")
ROWS = ("z", "y", "core")


ROWS_BY_COLS = (((1,), (0,)), ((), ()))
ROWS_BY_ROWS = (((1,), (1,)), ((), ()))
COLS_BY_COLS = (((0,), (0,)), ((), ()))

LEFT = (0, 0, 1, 0, 2, 1)
RIGHT = (0, 1, 0, 2, 0, 1)


def dot(a, b, dims=ROWS_BY_COLS):
    return lax.dot_general(a, b, dims, precision=HIGHEST, preferred_element_type=jnp.float32)


def split(x):
    first = x.astype(jnp.bfloat16)
    rest = x - first.astype(jnp.float32)
    second = rest.astype(jnp.bfloat16)
    return first, second, (rest - second.astype(jnp.float32)).astype(jnp.bfloat16)


def stack_rows(x, order):
    parts = split(x)
    return jnp.concatenate([parts[i] for i in order], axis=0)


def by_parts(x, parts):
    n = x.shape[0]
    lhs = jnp.concatenate(split(x), axis=0)
    r0 = jnp.dot(lhs, parts[0], preferred_element_type=jnp.float32)
    r1 = jnp.dot(lhs[: 2 * n], parts[1], preferred_element_type=jnp.float32)
    r2 = jnp.dot(lhs[:n], parts[2], preferred_element_type=jnp.float32)
    return r0[:n] + ((r0[n : 2 * n] + r1[:n]) + (r0[2 * n :] + r1[n:] + r2))


def by_factor(factor, x):
    size = x.shape[0]
    first, second, third = [t.astype(jnp.float32) for t in split(factor)]
    group = lax.broadcasted_iota(jnp.int32, factor.shape, 1) // size
    left = jnp.where(group == 0, 0.0, jnp.where(group == 3, second, first))
    right = jnp.where(group == 0, 0.0, jnp.where(group == 3, second, jnp.where(group == 2, third, first)))
    lhs = jnp.concatenate([left, right], axis=1).astype(jnp.bfloat16)
    return jnp.dot(lhs, stack_rows(x, (0, 0, 1, 0, 0, 2, 0, 1)), preferred_element_type=jnp.float32)


def by_columns(x, y):
    return lax.dot_general(
        stack_rows(x, LEFT), stack_rows(y, RIGHT), COLS_BY_COLS, preferred_element_type=jnp.float32
    )


def inverse_factor(square, size):
    blocks = size // SUB
    row = lax.broadcasted_iota(jnp.int32, (SUB, LANES), 0)
    lane = lax.broadcasted_iota(jnp.int32, (SUB, LANES), 1)

    def spread(tile, r):
        return jnp.broadcast_to(tile[r : r + 1, :], (SUB, LANES))

    rows = []
    for q in range(blocks):
        unit = jnp.where(lane % size == row + SUB * q, 1.0, 0.0)
        rows.append(jnp.where(lane < size, square[SUB * q : SUB * q + SUB, :], unit))
    pivots = [jnp.zeros((SUB, LANES), jnp.float32) for _ in range(blocks)]
    cols = {}

    def take(first):
        for j in range(first, min(first + PANEL, size)):
            for q in range(j // SUB, blocks):
                cols[j, q] = jnp.broadcast_to(rows[q][:, j : j + 1], (SUB, LANES))

    take(0)
    pivot = spread(cols[0, 0], 0)
    taken = PANEL
    for k in range(size):
        if k + EARLY == taken and taken < size:
            take(taken)
            taken += PANEL
        kq, kr = divmod(k, SUB)
        rough = pl.reciprocal(pivot, approx=True)
        near_one = pivot * rough
        recip = rough * (2.0 - near_one)
        pivots[kq] = jnp.where(row == kr, pivot, pivots[kq])
        if k + 1 < size:
            nq, nr = divmod(k + 1, SUB)
            beside = spread(cols[k, nq], nr)
            square_rough = beside * (beside * rough)
            pivot = spread(cols[k + 1, nq], nr) - square_rough * (2.0 - near_one)
        lower = {q: cols[k, q] for q in range(kq, blocks)}
        lower[kq] = jnp.where(row > kr, lower[kq], 0.0)
        lower = {q: t * recip for q, t in lower.items()}
        for j in range(k + 1, min(taken, size)):
            jq, jr = divmod(j, SUB)
            factor = spread(cols[k, jq], jr)
            for q in range(jq, blocks):
                cols[j, q] = cols[j, q] - lower[q] * factor
        above = spread(rows[kq], kr)
        for q in range(kq, blocks):
            rows[q] = rows[q] - lower[q] * above
    return jnp.concatenate([t * lax.rsqrt(p) for t, p in zip(rows, pivots)], axis=0)


def chosen_here(pivots_ref, width):
    place = lax.axis_index(ROWS + ("panel",))
    lane = lax.broadcasted_iota(jnp.int32, (LANES, LANES), 1).astype(jnp.float32)
    chosen = []
    for first in range(0, width, LANES):
        chosen.append(jnp.zeros((LANES, LANES), jnp.float32))
    for group in range(pivots_ref.shape[0]):
        here = (pivots_ref[group : group + 1, :] - place * width).astype(jnp.float32)
        here = jnp.broadcast_to(here, (LANES, LANES)).T
        for i in range(len(chosen)):
            chosen[i] = jnp.where(here == lane + float(i * LANES), 1.0, chosen[i])
    return jnp.concatenate([jnp.max(c, axis=0, keepdims=True) for c in chosen], axis=1)


def pack_kernel(cols_ref, pivots_ref, out_ref):
    far, subs, width = out_ref.shape
    size = cols_ref.shape[0]
    each = size // far // subs
    row = lax.broadcasted_iota(jnp.int32, (size, size), 0)
    lane = lax.broadcasted_iota(jnp.int32, (size, size), 1)
    high, middle, low = split(cols_ref[...])
    chosen = chosen_here(pivots_ref, cols_ref.shape[1]).astype(jnp.bfloat16)
    first = jnp.concatenate([high, high * chosen], axis=0)
    second = jnp.concatenate([middle, middle * chosen], axis=0)

    def product(x, y):
        return lax.dot_general(x, y, ROWS_BY_ROWS, preferred_element_type=jnp.float32)

    mirrored = product(first, low) + product(first, middle)
    plain = product(second, middle) + product(first, high)
    gram_half, core_half = mirrored[:size], mirrored[size:]
    turned = jnp.where(row <= lane, gram_half, core_half).T
    packed = jnp.where(row >= lane, plain[:size] + gram_half, plain[size:] + core_half) + turned
    core_diagonal = plain[size:] + 2.0 * core_half
    diagonal = jnp.sum(jnp.where(row == lane, core_diagonal, 0.0), axis=1, keepdims=True)
    spare = width - each * size
    spare_lane = lax.broadcasted_iota(jnp.int32, (far, spare), 1)
    for r in range(subs):
        tail = jnp.zeros((far, spare), jnp.float32)
        for h in range(each):
            at = (r * each + h) * far
            out_ref[:, r, h * size : (h + 1) * size] = packed[at : at + far, :]
            tail = jnp.where(spare_lane == h, diagonal[at : at + far, :], tail)
        out_ref[:, r, each * size :] = tail


def pack(cols, pivots, far):
    size = cols.shape[0]
    each = size // far // SUBS
    return pl.pallas_call(
        pack_kernel,
        out_shape=jax.ShapeDtypeStruct((far, SUBS, each * size + LANES), jnp.float32),
        in_specs=[pl.BlockSpec(memory_space=pltpu.VMEM)] * 2,
        out_specs=pl.BlockSpec(memory_space=pltpu.VMEM),
        compiler_params=pltpu.CompilerParams(vmem_limit_bytes=32 * 2**20),
        name="pack",
    )(cols, pivots.reshape(-1, LANES))


def solve_kernel(voxels, packed_ref, start_ref, cols_ref, out_ref, work, gram, gram_parts, inverse_parts, cols_parts):
    size = cols_ref.shape[0]
    rank = start_ref.shape[0]
    far, subs, width = packed_ref.shape
    each = size // far // subs
    every_row = lax.broadcasted_iota(jnp.int32, (size, size), 0)
    every_lane = lax.broadcasted_iota(jnp.int32, (size, size), 1)
    rows, diagonal = [], []
    for r in range(subs):
        tail = packed_ref[:, r, each * size :]
        for h in range(each):
            rows.append(packed_ref[:, r, h * size : (h + 1) * size])
            diagonal.append(tail[:, h : h + 1])
    packed = jnp.concatenate(rows, axis=0)
    flipped = packed.T
    gram[...] = jnp.where(every_row >= every_lane, packed, flipped) * (1.0 / voxels)
    core = jnp.where(every_row < every_lane, packed, flipped)
    core = jnp.where(every_row == every_lane, jnp.concatenate(diagonal, axis=0), core) * (1.0 / size)
    core = core + jnp.where(every_row == every_lane, CORE_SHIFT, 0.0)
    work[...] = core

    lane = lax.broadcasted_iota(jnp.int32, (BLOCK, size), 1)
    row = lax.broadcasted_iota(jnp.int32, (BLOCK, size), 0)

    def update(scaled, base):
        keep_row = (every_row < base) | (every_row >= base + BLOCK)
        keep_lane = (every_lane < base) | (every_lane >= base + BLOCK)
        work[...] = jnp.where(keep_row & keep_lane, work[...], 0.0) - by_columns(scaled, scaled)

    def sweep(step, carry):
        scaled, corner = carry
        base = pl.multiple_of(step * BLOCK, BLOCK)
        rows_here = pl.ds(base, BLOCK)
        factor = inverse_factor(corner, BLOCK)
        update(scaled, base - BLOCK)
        band = work[rows_here, :]
        inside = (lane >= base) & (lane < base + BLOCK)
        band = jnp.where(inside, jnp.where(lane - base == row, -1.0, 0.0), band)
        then = jnp.minimum(base + BLOCK, size - BLOCK)
        tile = pl.multiple_of(then // LANES * LANES, LANES)
        shift = LANES - lax.rem(then, LANES)
        own = band[:, :LANES]
        for t in range(LANES, size, LANES):
            own = jnp.where(then >= t, band[:, t : t + LANES], own)
        own = pltpu.roll(own, shift, axis=1)
        corner = pltpu.roll(work[pl.ds(pl.multiple_of(then, BLOCK), BLOCK), pl.ds(tile, LANES)], shift, axis=1)
        own = by_factor(factor, own)
        corner = corner - by_columns(own, own)[:BLOCK, :]
        scaled = by_factor(factor, band)
        for i, part in enumerate(split(cols_ref[rows_here, :])):
            cols_parts[i, rows_here, :] = part
        for i, part in enumerate(split(gram[rows_here, :])):
            gram_parts[i, rows_here, :] = part
        return scaled, corner

    nothing = jnp.zeros((BLOCK, size), jnp.float32)
    last = size // BLOCK - 1
    carry = lax.fori_loop(0, last, sweep, (nothing, core[:BLOCK, :LANES]))
    scaled, _ = sweep(jnp.int32(last), carry)
    keep = (every_row < size - BLOCK) & (every_lane < size - BLOCK)
    kept = jnp.where(keep, work[...], 0.0)
    for i, part in enumerate(split(by_columns(scaled, scaled) - kept)):
        inverse_parts[i] = part

    def by(ref, x):
        return by_parts(x, (ref[0], ref[1], ref[2]))

    def factor_of(image, pushed):
        small = dot(image, pushed, ROWS_BY_ROWS)
        small = jnp.concatenate([small, jnp.zeros((rank, LANES - rank), jnp.float32)], axis=1)
        return inverse_factor(small, rank)

    def iterate(step, carry):
        image, pushed = carry
        factor = factor_of(image, pushed)
        top = jnp.max(jnp.max(jnp.abs(pushed), axis=0, keepdims=True), axis=1, keepdims=True)
        ahead = by(inverse_parts, pushed * (1.0 / top))
        ahead_pushed = by(gram_parts, ahead)
        scaled_factor = factor * top
        return by_factor(scaled_factor, ahead), by_factor(scaled_factor, ahead_pushed)

    pushed = by(gram_parts, start_ref[...])
    image = dot(dot(pushed, scaled, ROWS_BY_ROWS), scaled) - by_parts(pushed, split(kept))
    image, pushed = lax.fori_loop(0, ITERS - 1, iterate, (image, by(gram_parts, image)))
    volumes = by(cols_parts, image)
    out_ref[...] = by_factor(factor_of(image, pushed), volumes)


def solve(packed, start, cols, voxels):
    size, width = cols.shape
    rank = start.shape[0]
    return pl.pallas_call(
        functools.partial(solve_kernel, voxels),
        out_shape=jax.ShapeDtypeStruct((rank, width), jnp.float32),
        in_specs=[pl.BlockSpec(memory_space=pltpu.VMEM)] * 3,
        out_specs=pl.BlockSpec(memory_space=pltpu.VMEM),
        scratch_shapes=[
            pltpu.VMEM((size, size), jnp.float32),
            pltpu.VMEM((size, size), jnp.float32),
            pltpu.VMEM((3, size, size), jnp.bfloat16),
            pltpu.VMEM((3, size, size), jnp.bfloat16),
            pltpu.VMEM((3, size, width), jnp.bfloat16),
        ],
        compiler_params=pltpu.CompilerParams(vmem_limit_bytes=32 * 2**20),
        name="solve",
    )(packed, start, cols)


def sum_everywhere(pieces):
    far, subs, width = pieces.shape
    near = lax.axis_size(NEAR)
    piece = jnp.sum(lax.all_to_all(pieces, FAR, 0, 0, tiled=True), axis=0)
    copies = jnp.broadcast_to(piece[None], (near, subs, width))
    piece = jnp.sum(lax.all_to_all(copies, NEAR, 0, 0, tiled=True), axis=0)
    copies = jnp.broadcast_to(piece[None], (far, subs, width))
    return lax.all_to_all(copies, FAR, 0, 0, tiled=True)


def body(columns, pivots, start):
    width = columns.shape[1] // lax.axis_size("panel")
    voxels = width * lax.axis_size(ROWS + ("panel",))
    cols = lax.all_to_all(columns, "panel", 1, 0, tiled=True)
    packed = sum_everywhere(pack(cols, pivots, lax.axis_size(FAR)))
    return solve(packed, start.T, cols, voxels)


def solution(mesh):
    fine = Mesh(mesh.devices.reshape(8, 8, 2, 4), ROWS + ("panel",))
    return jax.shard_map(
        body,
        mesh=fine,
        in_specs=(P("panel", ROWS), P(), P()),
        out_specs=P(None, ROWS + ("panel",)),
        check_vma=False,
    )
```

```python
import functools

import jax
import jax.numpy as jnp
from jax import lax
from jax.experimental import pallas as pl
from jax.experimental.pallas import tpu as pltpu
from jax.sharding import Mesh, PartitionSpec as P

ITERS = 3
CORE_SHIFT = 0.1
HIGHEST = lax.Precision.HIGHEST
SUB = 8
LANES = 128
BLOCK = 32
PANEL = 16
EARLY = 4
SUBS = 1

FAR = ("panel", "y")
NEAR = ("core", "z")
ROWS = ("z", "y", "core")


ROWS_BY_COLS = (((1,), (0,)), ((), ()))
ROWS_BY_ROWS = (((1,), (1,)), ((), ()))
COLS_BY_COLS = (((0,), (0,)), ((), ()))

LEFT = (0, 0, 1, 0, 2, 1)
RIGHT = (0, 1, 0, 2, 0, 1)


def dot(a, b, dims=ROWS_BY_COLS):
    return lax.dot_general(a, b, dims, precision=HIGHEST, preferred_element_type=jnp.float32)


def split(x):
    first = x.astype(jnp.bfloat16)
    rest = x - first.astype(jnp.float32)
    second = rest.astype(jnp.bfloat16)
    return first, second, (rest - second.astype(jnp.float32)).astype(jnp.bfloat16)


def stack_rows(x, order):
    parts = split(x)
    return jnp.concatenate([parts[i] for i in order], axis=0)


def by_parts(x, parts):
    n = x.shape[0]
    lhs = jnp.concatenate(split(x), axis=0)
    r0 = jnp.dot(lhs, parts[0], preferred_element_type=jnp.float32)
    r1 = jnp.dot(lhs[: 2 * n], parts[1], preferred_element_type=jnp.float32)
    r2 = jnp.dot(lhs[:n], parts[2], preferred_element_type=jnp.float32)
    return r0[:n] + ((r0[n : 2 * n] + r1[:n]) + (r0[2 * n :] + r1[n:] + r2))


def by_factor(factor, x):
    size = x.shape[0]
    first, second, third = [t.astype(jnp.float32) for t in split(factor)]
    group = lax.broadcasted_iota(jnp.int32, factor.shape, 1) // size
    left = jnp.where(group == 0, 0.0, jnp.where(group == 3, second, first))
    right = jnp.where(group == 0, 0.0, jnp.where(group == 3, second, jnp.where(group == 2, third, first)))
    lhs = jnp.concatenate([left, right], axis=1).astype(jnp.bfloat16)
    return jnp.dot(lhs, stack_rows(x, (0, 0, 1, 0, 0, 2, 0, 1)), preferred_element_type=jnp.float32)


def by_columns(x, y):
    return lax.dot_general(
        stack_rows(x, LEFT), stack_rows(y, RIGHT), COLS_BY_COLS, preferred_element_type=jnp.float32
    )


def inverse_factor(square, size):
    blocks = size // SUB
    row = lax.broadcasted_iota(jnp.int32, (SUB, LANES), 0)
    lane = lax.broadcasted_iota(jnp.int32, (SUB, LANES), 1)

    def spread(tile, r):
        return jnp.broadcast_to(tile[r : r + 1, :], (SUB, LANES))

    rows = []
    for q in range(blocks):
        unit = jnp.where(lane % size == row + SUB * q, 1.0, 0.0)
        rows.append(jnp.where(lane < size, square[SUB * q : SUB * q + SUB, :], unit))
    pivots = [jnp.zeros((SUB, LANES), jnp.float32) for _ in range(blocks)]
    cols = {}

    def take(first):
        for j in range(first, min(first + PANEL, size)):
            for q in range(j // SUB, blocks):
                cols[j, q] = jnp.broadcast_to(rows[q][:, j : j + 1], (SUB, LANES))

    take(0)
    pivot = spread(cols[0, 0], 0)
    taken = PANEL
    for k in range(size):
        if k + EARLY == taken and taken < size:
            take(taken)
            taken += PANEL
        kq, kr = divmod(k, SUB)
        rough = pl.reciprocal(pivot, approx=True)
        near_one = pivot * rough
        recip = rough * (2.0 - near_one)
        pivots[kq] = jnp.where(row == kr, pivot, pivots[kq])
        if k + 1 < size:
            nq, nr = divmod(k + 1, SUB)
            beside = spread(cols[k, nq], nr)
            square_rough = beside * (beside * rough)
            pivot = spread(cols[k + 1, nq], nr) - square_rough * (2.0 - near_one)
        lower = {q: cols[k, q] for q in range(kq, blocks)}
        lower[kq] = jnp.where(row > kr, lower[kq], 0.0)
        lower = {q: t * recip for q, t in lower.items()}
        for j in range(k + 1, min(taken, size)):
            jq, jr = divmod(j, SUB)
            factor = spread(cols[k, jq], jr)
            for q in range(jq, blocks):
                cols[j, q] = cols[j, q] - lower[q] * factor
        above = spread(rows[kq], kr)
        for q in range(kq, blocks):
            rows[q] = rows[q] - lower[q] * above
    return jnp.concatenate([t * lax.rsqrt(p) for t, p in zip(rows, pivots)], axis=0)


def chosen_here(pivots_ref, width):
    place = lax.axis_index(ROWS + ("panel",))
    lane = lax.broadcasted_iota(jnp.int32, (LANES, LANES), 1).astype(jnp.float32)
    chosen = []
    for first in range(0, width, LANES):
        chosen.append(jnp.zeros((LANES, LANES), jnp.float32))
    for group in range(pivots_ref.shape[0]):
        here = (pivots_ref[group : group + 1, :] - place * width).astype(jnp.float32)
        here = jnp.broadcast_to(here, (LANES, LANES)).T
        for i in range(len(chosen)):
            chosen[i] = jnp.where(here == lane + float(i * LANES), 1.0, chosen[i])
    return jnp.concatenate([jnp.max(c, axis=0, keepdims=True) for c in chosen], axis=1)


def pack_kernel(cols_ref, pivots_ref, out_ref):
    far, subs, width = out_ref.shape
    size = cols_ref.shape[0]
    each = size // far // subs
    row = lax.broadcasted_iota(jnp.int32, (size, size), 0)
    lane = lax.broadcasted_iota(jnp.int32, (size, size), 1)
    high, middle, low = split(cols_ref[...])
    chosen = chosen_here(pivots_ref, cols_ref.shape[1]).astype(jnp.bfloat16)
    first = jnp.concatenate([high, high * chosen], axis=0)
    second = jnp.concatenate([middle, middle * chosen], axis=0)

    def product(x, y):
        return lax.dot_general(x, y, ROWS_BY_ROWS, preferred_element_type=jnp.float32)

    mirrored = product(first, low) + product(first, middle)
    plain = product(second, middle) + product(first, high)
    gram_half, core_half = mirrored[:size], mirrored[size:]
    turned = jnp.where(row <= lane, gram_half, core_half).T
    packed = jnp.where(row >= lane, plain[:size] + gram_half, plain[size:] + core_half) + turned
    core_diagonal = plain[size:] + 2.0 * core_half
    diagonal = jnp.sum(jnp.where(row == lane, core_diagonal, 0.0), axis=1, keepdims=True)
    spare = width - each * size
    spare_lane = lax.broadcasted_iota(jnp.int32, (far, spare), 1)
    for r in range(subs):
        tail = jnp.zeros((far, spare), jnp.float32)
        for h in range(each):
            at = (r * each + h) * far
            out_ref[:, r, h * size : (h + 1) * size] = packed[at : at + far, :]
            tail = jnp.where(spare_lane == h, diagonal[at : at + far, :], tail)
        out_ref[:, r, each * size :] = tail


def pack(cols, pivots, far):
    size = cols.shape[0]
    each = size // far // SUBS
    return pl.pallas_call(
        pack_kernel,
        out_shape=jax.ShapeDtypeStruct((far, SUBS, each * size + LANES), jnp.float32),
        in_specs=[pl.BlockSpec(memory_space=pltpu.VMEM)] * 2,
        out_specs=pl.BlockSpec(memory_space=pltpu.VMEM),
        compiler_params=pltpu.CompilerParams(vmem_limit_bytes=32 * 2**20),
        name="pack",
    )(cols, pivots.reshape(-1, LANES))


def solve_kernel(voxels, packed_ref, start_ref, cols_ref, out_ref, work, gram, gram_parts, inverse_parts, cols_parts):
    size = cols_ref.shape[0]
    rank = start_ref.shape[0]
    far, subs, width = packed_ref.shape
    each = size // far // subs
    every_row = lax.broadcasted_iota(jnp.int32, (size, size), 0)
    every_lane = lax.broadcasted_iota(jnp.int32, (size, size), 1)
    rows, diagonal = [], []
    for r in range(subs):
        tail = packed_ref[:, r, each * size :]
        for h in range(each):
            rows.append(packed_ref[:, r, h * size : (h + 1) * size])
            diagonal.append(tail[:, h : h + 1])
    packed = jnp.concatenate(rows, axis=0)
    flipped = packed.T
    gram[...] = jnp.where(every_row >= every_lane, packed, flipped) * (1.0 / voxels)
    core = jnp.where(every_row < every_lane, packed, flipped)
    core = jnp.where(every_row == every_lane, jnp.concatenate(diagonal, axis=0), core) * (1.0 / size)
    core = core + jnp.where(every_row == every_lane, CORE_SHIFT, 0.0)
    work[...] = core

    lane = lax.broadcasted_iota(jnp.int32, (BLOCK, size), 1)
    row = lax.broadcasted_iota(jnp.int32, (BLOCK, size), 0)

    def update(scaled, base):
        keep_row = (every_row < base) | (every_row >= base + BLOCK)
        keep_lane = (every_lane < base) | (every_lane >= base + BLOCK)
        work[...] = jnp.where(keep_row & keep_lane, work[...], 0.0) - by_columns(scaled, scaled)

    def sweep(step, carry):
        scaled, corner = carry
        base = pl.multiple_of(step * BLOCK, BLOCK)
        rows_here = pl.ds(base, BLOCK)
        factor = inverse_factor(corner, BLOCK)
        update(scaled, base - BLOCK)
        band = work[rows_here, :]
        inside = (lane >= base) & (lane < base + BLOCK)
        band = jnp.where(inside, jnp.where(lane - base == row, -1.0, 0.0), band)
        then = jnp.minimum(base + BLOCK, size - BLOCK)
        tile = pl.multiple_of(then // LANES * LANES, LANES)
        shift = LANES - lax.rem(then, LANES)
        own = band[:, :LANES]
        for t in range(LANES, size, LANES):
            own = jnp.where(then >= t, band[:, t : t + LANES], own)
        own = pltpu.roll(own, shift, axis=1)
        corner = pltpu.roll(work[pl.ds(pl.multiple_of(then, BLOCK), BLOCK), pl.ds(tile, LANES)], shift, axis=1)
        own = by_factor(factor, own)
        corner = corner - by_columns(own, own)[:BLOCK, :]
        scaled = by_factor(factor, band)
        for i, part in enumerate(split(cols_ref[rows_here, :])):
            cols_parts[i, rows_here, :] = part
        for i, part in enumerate(split(gram[rows_here, :])):
            gram_parts[i, rows_here, :] = part
        return scaled, corner

    nothing = jnp.zeros((BLOCK, size), jnp.float32)
    last = size // BLOCK - 1
    carry = lax.fori_loop(0, last, sweep, (nothing, core[:BLOCK, :LANES]))
    scaled, _ = sweep(jnp.int32(last), carry)
    keep = (every_row < size - BLOCK) & (every_lane < size - BLOCK)
    kept = jnp.where(keep, work[...], 0.0)
    for i, part in enumerate(split(by_columns(scaled, scaled) - kept)):
        inverse_parts[i] = part

    def by(ref, x):
        return by_parts(x, (ref[0], ref[1], ref[2]))

    def factor_of(image, pushed):
        small = dot(image, pushed, ROWS_BY_ROWS)
        small = jnp.concatenate([small, jnp.zeros((rank, LANES - rank), jnp.float32)], axis=1)
        return inverse_factor(small, rank)

    def iterate(step, carry):
        image, pushed = carry
        factor = factor_of(image, pushed)
        top = jnp.max(jnp.max(jnp.abs(pushed), axis=0, keepdims=True), axis=1, keepdims=True)
        ahead = by(inverse_parts, pushed * (1.0 / top))
        ahead_pushed = by(gram_parts, ahead)
        scaled_factor = factor * top
        return by_factor(scaled_factor, ahead), by_factor(scaled_factor, ahead_pushed)

    pushed = by(gram_parts, start_ref[...])
    image = dot(dot(pushed, scaled, ROWS_BY_ROWS), scaled) - by_parts(pushed, split(kept))
    image, pushed = lax.fori_loop(0, ITERS - 1, iterate, (image, by(gram_parts, image)))
    volumes = by(cols_parts, image)
    out_ref[...] = by_factor(factor_of(image, pushed), volumes)


def solve(packed, start, cols, voxels):
    size, width = cols.shape
    rank = start.shape[0]
    return pl.pallas_call(
        functools.partial(solve_kernel, voxels),
        out_shape=jax.ShapeDtypeStruct((rank, width), jnp.float32),
        in_specs=[pl.BlockSpec(memory_space=pltpu.VMEM)] * 3,
        out_specs=pl.BlockSpec(memory_space=pltpu.VMEM),
        scratch_shapes=[
            pltpu.VMEM((size, size), jnp.float32),
            pltpu.VMEM((size, size), jnp.float32),
            pltpu.VMEM((3, size, size), jnp.bfloat16),
            pltpu.VMEM((3, size, size), jnp.bfloat16),
            pltpu.VMEM((3, size, width), jnp.bfloat16),
        ],
        compiler_params=pltpu.CompilerParams(vmem_limit_bytes=32 * 2**20),
        name="solve",
    )(packed, start, cols)


def sum_everywhere(pieces):
    far, subs, width = pieces.shape
    near = lax.axis_size(NEAR)
    piece = jnp.sum(lax.all_to_all(pieces, FAR, 0, 0, tiled=True), axis=0)
    copies = jnp.broadcast_to(piece[None], (near, subs, width))
    piece = jnp.sum(lax.all_to_all(copies, NEAR, 0, 0, tiled=True), axis=0)
    copies = jnp.broadcast_to(piece[None], (far, subs, width))
    return lax.all_to_all(copies, FAR, 0, 0, tiled=True)


def body(columns, pivots, start):
    width = columns.shape[1] // lax.axis_size("panel")
    voxels = width * lax.axis_size(ROWS + ("panel",))
    cols = lax.all_to_all(columns, "panel", 1, 0, tiled=True)
    packed = sum_everywhere(pack(cols, pivots, lax.axis_size(FAR)))
    return solve(packed, start.T, cols, voxels)


def solution(mesh):
    fine = Mesh(mesh.devices.reshape(8, 8, 2, 4), ROWS + ("panel",))
    return jax.shard_map(
        body,
        mesh=fine,
        in_specs=(P("panel", ROWS), P(), P()),
        out_specs=P(None, ROWS + ("panel",)),
        check_vma=False,
    )
```

```python
import functools

import jax
import jax.numpy as jnp
from jax import lax
from jax.experimental import pallas as pl
from jax.experimental.pallas import tpu as pltpu
from jax.sharding import Mesh, PartitionSpec as P

ITERS = 3
CORE_SHIFT = 0.1
HIGHEST = lax.Precision.HIGHEST
SUB = 8
LANES = 128
BLOCK = 32
PANEL = 16
EARLY = 4
SUBS = 1

FAR = ("panel", "z")
NEAR = ("core", "y")
ROWS = ("z", "y", "core")


ROWS_BY_COLS = (((1,), (0,)), ((), ()))
ROWS_BY_ROWS = (((1,), (1,)), ((), ()))
COLS_BY_COLS = (((0,), (0,)), ((), ()))

LEFT = (0, 0, 1, 0, 2, 1)
RIGHT = (0, 1, 0, 2, 0, 1)


def dot(a, b, dims=ROWS_BY_COLS):
    return lax.dot_general(a, b, dims, precision=HIGHEST, preferred_element_type=jnp.float32)


def split(x):
    first = x.astype(jnp.bfloat16)
    rest = x - first.astype(jnp.float32)
    second = rest.astype(jnp.bfloat16)
    return first, second, (rest - second.astype(jnp.float32)).astype(jnp.bfloat16)


def stack_rows(x, order):
    parts = split(x)
    return jnp.concatenate([parts[i] for i in order], axis=0)


def by_parts(x, parts):
    n = x.shape[0]
    lhs = jnp.concatenate(split(x), axis=0)
    r0 = jnp.dot(lhs, parts[0], preferred_element_type=jnp.float32)
    r1 = jnp.dot(lhs[: 2 * n], parts[1], preferred_element_type=jnp.float32)
    r2 = jnp.dot(lhs[:n], parts[2], preferred_element_type=jnp.float32)
    return r0[:n] + ((r0[n : 2 * n] + r1[:n]) + (r0[2 * n :] + r1[n:] + r2))


def by_factor(factor, x):
    size = x.shape[0]
    first, second, third = [t.astype(jnp.float32) for t in split(factor)]
    group = lax.broadcasted_iota(jnp.int32, factor.shape, 1) // size
    left = jnp.where(group == 0, 0.0, jnp.where(group == 3, second, first))
    right = jnp.where(group == 0, 0.0, jnp.where(group == 3, second, jnp.where(group == 2, third, first)))
    lhs = jnp.concatenate([left, right], axis=1).astype(jnp.bfloat16)
    return jnp.dot(lhs, stack_rows(x, (0, 0, 1, 0, 0, 2, 0, 1)), preferred_element_type=jnp.float32)


def by_columns(x, y):
    return lax.dot_general(
        stack_rows(x, LEFT), stack_rows(y, RIGHT), COLS_BY_COLS, preferred_element_type=jnp.float32
    )


def inverse_factor(square, size):
    blocks = size // SUB
    row = lax.broadcasted_iota(jnp.int32, (SUB, LANES), 0)
    lane = lax.broadcasted_iota(jnp.int32, (SUB, LANES), 1)

    def spread(tile, r):
        return jnp.broadcast_to(tile[r : r + 1, :], (SUB, LANES))

    rows = []
    for q in range(blocks):
        unit = jnp.where(lane % size == row + SUB * q, 1.0, 0.0)
        rows.append(jnp.where(lane < size, square[SUB * q : SUB * q + SUB, :], unit))
    pivots = [jnp.zeros((SUB, LANES), jnp.float32) for _ in range(blocks)]
    cols = {}

    def take(first):
        for j in range(first, min(first + PANEL, size)):
            for q in range(j // SUB, blocks):
                cols[j, q] = jnp.broadcast_to(rows[q][:, j : j + 1], (SUB, LANES))

    take(0)
    pivot = spread(cols[0, 0], 0)
    taken = PANEL
    for k in range(size):
        if k + EARLY == taken and taken < size:
            take(taken)
            taken += PANEL
        kq, kr = divmod(k, SUB)
        rough = pl.reciprocal(pivot, approx=True)
        near_one = pivot * rough
        recip = rough * (2.0 - near_one)
        pivots[kq] = jnp.where(row == kr, pivot, pivots[kq])
        if k + 1 < size:
            nq, nr = divmod(k + 1, SUB)
            beside = spread(cols[k, nq], nr)
            square_rough = beside * (beside * rough)
            pivot = spread(cols[k + 1, nq], nr) - square_rough * (2.0 - near_one)
        lower = {q: cols[k, q] for q in range(kq, blocks)}
        lower[kq] = jnp.where(row > kr, lower[kq], 0.0)
        lower = {q: t * recip for q, t in lower.items()}
        for j in range(k + 1, min(taken, size)):
            jq, jr = divmod(j, SUB)
            factor = spread(cols[k, jq], jr)
            for q in range(jq, blocks):
                cols[j, q] = cols[j, q] - lower[q] * factor
        above = spread(rows[kq], kr)
        for q in range(kq, blocks):
            rows[q] = rows[q] - lower[q] * above
    return jnp.concatenate([t * lax.rsqrt(p) for t, p in zip(rows, pivots)], axis=0)


def chosen_here(pivots_ref, width):
    place = lax.axis_index(ROWS + ("panel",))
    lane = lax.broadcasted_iota(jnp.int32, (LANES, LANES), 1).astype(jnp.float32)
    chosen = []
    for first in range(0, width, LANES):
        chosen.append(jnp.zeros((LANES, LANES), jnp.float32))
    for group in range(pivots_ref.shape[0]):
        here = (pivots_ref[group : group + 1, :] - place * width).astype(jnp.float32)
        here = jnp.broadcast_to(here, (LANES, LANES)).T
        for i in range(len(chosen)):
            chosen[i] = jnp.where(here == lane + float(i * LANES), 1.0, chosen[i])
    return jnp.concatenate([jnp.max(c, axis=0, keepdims=True) for c in chosen], axis=1)


def pack_kernel(cols_ref, pivots_ref, out_ref):
    far, subs, width = out_ref.shape
    size = cols_ref.shape[0]
    each = size // far // subs
    row = lax.broadcasted_iota(jnp.int32, (size, size), 0)
    lane = lax.broadcasted_iota(jnp.int32, (size, size), 1)
    high, middle, low = split(cols_ref[...])
    chosen = chosen_here(pivots_ref, cols_ref.shape[1]).astype(jnp.bfloat16)
    first = jnp.concatenate([high, high * chosen], axis=0)
    second = jnp.concatenate([middle, middle * chosen], axis=0)

    def product(x, y):
        return lax.dot_general(x, y, ROWS_BY_ROWS, preferred_element_type=jnp.float32)

    mirrored = product(first, low) + product(first, middle)
    plain = product(second, middle) + product(first, high)
    gram_half, core_half = mirrored[:size], mirrored[size:]
    turned = jnp.where(row <= lane, gram_half, core_half).T
    packed = jnp.where(row >= lane, plain[:size] + gram_half, plain[size:] + core_half) + turned
    core_diagonal = plain[size:] + 2.0 * core_half
    diagonal = jnp.sum(jnp.where(row == lane, core_diagonal, 0.0), axis=1, keepdims=True)
    spare = width - each * size
    spare_lane = lax.broadcasted_iota(jnp.int32, (far, spare), 1)
    for r in range(subs):
        tail = jnp.zeros((far, spare), jnp.float32)
        for h in range(each):
            at = (r * each + h) * far
            out_ref[:, r, h * size : (h + 1) * size] = packed[at : at + far, :]
            tail = jnp.where(spare_lane == h, diagonal[at : at + far, :], tail)
        out_ref[:, r, each * size :] = tail


def pack(cols, pivots, far):
    size = cols.shape[0]
    each = size // far // SUBS
    return pl.pallas_call(
        pack_kernel,
        out_shape=jax.ShapeDtypeStruct((far, SUBS, each * size + LANES), jnp.float32),
        in_specs=[pl.BlockSpec(memory_space=pltpu.VMEM)] * 2,
        out_specs=pl.BlockSpec(memory_space=pltpu.VMEM),
        compiler_params=pltpu.CompilerParams(vmem_limit_bytes=32 * 2**20),
        name="pack",
    )(cols, pivots.reshape(-1, LANES))


def solve_kernel(voxels, packed_ref, start_ref, cols_ref, out_ref, work, square, gram_parts, inverse_parts, cols_parts):
    size = cols_ref.shape[0]
    rank = start_ref.shape[0]
    far, subs, width = packed_ref.shape
    each = size // far // subs
    every_row = lax.broadcasted_iota(jnp.int32, (size, size), 0)
    every_lane = lax.broadcasted_iota(jnp.int32, (size, size), 1)
    rows, diagonal = [], []
    for r in range(subs):
        tail = packed_ref[:, r, each * size :]
        for h in range(each):
            rows.append(packed_ref[:, r, h * size : (h + 1) * size])
            diagonal.append(tail[:, h : h + 1])
    packed = jnp.concatenate(rows, axis=0)
    flipped = packed.T
    square[0] = packed
    square[1] = flipped
    core = jnp.where(every_row < every_lane, packed, flipped)
    core = jnp.where(every_row == every_lane, jnp.concatenate(diagonal, axis=0), core) * (1.0 / size)
    core = core + jnp.where(every_row == every_lane, CORE_SHIFT, 0.0)
    work[...] = core

    lane = lax.broadcasted_iota(jnp.int32, (BLOCK, size), 1)
    row = lax.broadcasted_iota(jnp.int32, (BLOCK, size), 0)

    def update(scaled, base):
        keep_row = (every_row < base) | (every_row >= base + BLOCK)
        keep_lane = (every_lane < base) | (every_lane >= base + BLOCK)
        work[...] = jnp.where(keep_row & keep_lane, work[...], 0.0) - by_columns(scaled, scaled)

    def sweep(step, carry):
        scaled, corner = carry
        base = pl.multiple_of(step * BLOCK, BLOCK)
        rows_here = pl.ds(base, BLOCK)
        factor = inverse_factor(corner, BLOCK)
        update(scaled, base - BLOCK)
        band = work[rows_here, :]
        inside = (lane >= base) & (lane < base + BLOCK)
        band = jnp.where(inside, jnp.where(lane - base == row, -1.0, 0.0), band)
        then = jnp.minimum(base + BLOCK, size - BLOCK)
        tile = pl.multiple_of(then // LANES * LANES, LANES)
        shift = LANES - lax.rem(then, LANES)
        own = band[:, :LANES]
        for t in range(LANES, size, LANES):
            own = jnp.where(then >= t, band[:, t : t + LANES], own)
        own = pltpu.roll(own, shift, axis=1)
        corner = pltpu.roll(work[pl.ds(pl.multiple_of(then, BLOCK), BLOCK), pl.ds(tile, LANES)], shift, axis=1)
        own = by_factor(factor, own)
        corner = corner - by_columns(own, own)[:BLOCK, :]
        scaled = by_factor(factor, band)
        for i, part in enumerate(split(cols_ref[rows_here, :])):
            cols_parts[i, rows_here, :] = part
        below = row + base >= lane
        gram = jnp.where(below, square[0, rows_here, :], square[1, rows_here, :]) * (1.0 / voxels)
        for i, part in enumerate(split(gram)):
            gram_parts[i, rows_here, :] = part
        return scaled, corner

    nothing = jnp.zeros((BLOCK, size), jnp.float32)
    last = size // BLOCK - 1
    carry = lax.fori_loop(0, last, sweep, (nothing, core[:BLOCK, :LANES]))
    scaled, _ = sweep(jnp.int32(last), carry)
    keep = (every_row < size - BLOCK) & (every_lane < size - BLOCK)
    kept = jnp.where(keep, work[...], 0.0)
    for i, part in enumerate(split(by_columns(scaled, scaled) - kept)):
        inverse_parts[i] = part

    def by(ref, x):
        return by_parts(x, (ref[0], ref[1], ref[2]))

    def factor_of(image, pushed):
        small = dot(image, pushed, ROWS_BY_ROWS)
        small = jnp.concatenate([small, jnp.zeros((rank, LANES - rank), jnp.float32)], axis=1)
        return inverse_factor(small, rank)

    def iterate(step, carry):
        image, pushed = carry
        factor = factor_of(image, pushed)
        top = jnp.max(jnp.max(jnp.abs(pushed), axis=0, keepdims=True), axis=1, keepdims=True)
        ahead = by(inverse_parts, pushed * (1.0 / top))
        ahead_pushed = by(gram_parts, ahead)
        scaled_factor = factor * top
        return by_factor(scaled_factor, ahead), by_factor(scaled_factor, ahead_pushed)

    pushed = by(gram_parts, start_ref[...])
    image = dot(dot(pushed, scaled, ROWS_BY_ROWS), scaled) - by_parts(pushed, split(kept))
    image, pushed = lax.fori_loop(0, ITERS - 1, iterate, (image, by(gram_parts, image)))
    volumes = by(cols_parts, image)
    out_ref[...] = by_factor(factor_of(image, pushed), volumes)


def solve(packed, start, cols, voxels):
    size, width = cols.shape
    rank = start.shape[0]
    return pl.pallas_call(
        functools.partial(solve_kernel, voxels),
        out_shape=jax.ShapeDtypeStruct((rank, width), jnp.float32),
        in_specs=[pl.BlockSpec(memory_space=pltpu.VMEM)] * 3,
        out_specs=pl.BlockSpec(memory_space=pltpu.VMEM),
        scratch_shapes=[
            pltpu.VMEM((size, size), jnp.float32),
            pltpu.VMEM((2, size, size), jnp.float32),
            pltpu.VMEM((3, size, size), jnp.bfloat16),
            pltpu.VMEM((3, size, size), jnp.bfloat16),
            pltpu.VMEM((3, size, width), jnp.bfloat16),
        ],
        compiler_params=pltpu.CompilerParams(vmem_limit_bytes=32 * 2**20),
        name="solve",
    )(packed, start, cols)


def sum_everywhere(pieces):
    far, subs, width = pieces.shape
    near = lax.axis_size(NEAR)
    piece = jnp.sum(lax.all_to_all(pieces, FAR, 0, 0, tiled=True), axis=0)
    copies = jnp.broadcast_to(piece[None], (near, subs, width))
    piece = jnp.sum(lax.all_to_all(copies, NEAR, 0, 0, tiled=True), axis=0)
    copies = jnp.broadcast_to(piece[None], (far, subs, width))
    return lax.all_to_all(copies, FAR, 0, 0, tiled=True)


def body(columns, pivots, start):
    width = columns.shape[1] // lax.axis_size("panel")
    voxels = width * lax.axis_size(ROWS + ("panel",))
    cols = lax.all_to_all(columns, "panel", 1, 0, tiled=True)
    packed = sum_everywhere(pack(cols, pivots, lax.axis_size(FAR)))
    return solve(packed, start.T, cols, voxels)


def solution(mesh):
    fine = Mesh(mesh.devices.reshape(8, 8, 2, 4), ROWS + ("panel",))
    return jax.shard_map(
        body,
        mesh=fine,
        in_specs=(P("panel", ROWS), P(), P()),
        out_specs=P(None, ROWS + ("panel",)),
        check_vma=False,
    )
```
